128 devices in a mesh: arc: 8 (over x, core), par: 16 (over y, z).
Axes of the slice: x: 4, y: 4, z: 4, core: 2. Of those that a mesh axis runs over, the one named last changes fastest.
Arguments:
- observations: float32 [2048, 65536], P('arc', 'par'), may hold values from -18 to 18
- arc_mask: int32 [16, 512], P('arc', 'par'), may hold values 0 or 1
- panel_owner: int32 [2], replicated, may hold values from 0 to 255, as said below
Outputs:
- info_rows: float32 [512, 65536], P('arc', 'par')
The draws below stay inside these ranges and needn't reach their ends.
Inputs may be any that keep to these rules, and one draw needn't show every extreme that they name: `panel_owner`: two different panel indices below 256; one of the two is always the last panel.
All inputs are finite; a program needn't handle non-finite values. No bound on the sum of `arc_mask` on one device may be relied on, other than what follows from the above.
Results may differ from the reference program's by a relative error of at most 0.002.
Values sent between devices are 32-bit elements; how exact they have to be, the bound alone decides.
A program may use at most 64 MiB of HBM per device.

```python
import math
import jax
import jax.numpy as jnp
from jax import lax

PANEL = 256
BLK = 128
ROWS = 2048
COLS = 65536


def draw_observations(key, part):
    row_key = jax.random.fold_in(key, 21)
    value_key = jax.random.fold_in(key, 23)
    common_key = jax.random.fold_in(key, 24)
    twin_key = jax.random.fold_in(key, 25)
    row_scale = jnp.exp(jax.random.uniform(row_key, (ROWS, 1), jnp.float32, math.log(0.3), math.log(3.0)))
    common = jnp.clip(jax.random.normal(common_key, (ROWS, 1), jnp.float32), -6.0, 6.0)
    twin_noise = jnp.clip(jax.random.normal(twin_key, (ROWS, 1), jnp.float32), -6.0, 6.0)
    values = jnp.clip(jax.random.normal(value_key, (ROWS, COLS), jnp.float32), -6.0, 6.0)
    share = 0.1
    base = math.sqrt(1.0 - share) * values + math.sqrt(share) * common
    twin_col = base[:, COLS - 2:COLS - 1] + 0.015 * twin_noise
    joined = jnp.concatenate([base[:, :COLS - 1], twin_col], 1)
    scaled = joined * row_scale
    return jnp.clip(scaled, -18.0, 18.0).astype(jnp.float32)


def draw_panel_owner(key, part):
    last_panel = COLS // PANEL - 1
    other_panel = jax.random.randint(jax.random.fold_in(key, 31), (), 0, last_panel)
    order_bit = jax.random.randint(jax.random.fold_in(key, 32), (), 0, 2)
    first_index = jnp.where(order_bit == 0, other_panel, last_panel)
    second_index = jnp.where(order_bit == 0, last_panel, other_panel)
    return jnp.stack([first_index, second_index]).astype(jnp.int32)


def set_ends(array, own_key, smallest, top_value):
    longest = array.shape.index(max(array.shape))
    spots = []
    for shift in (0, 1):
        where = [jax.random.randint(jax.random.fold_in(own_key, axis), (), 0, length) for axis, length in enumerate(array.shape)]
        where[longest] = (where[longest] + shift) % array.shape[longest]
        spots.append(tuple(where))
    return array.at[spots[0]].set(smallest).at[spots[1]].set(top_value)


def setup_inputs(seed: int = 0) -> dict:
    seeds = jax.random.split(jax.random.key(seed), 4)
    observations = draw_observations(jax.random.fold_in(seeds[3], 71), 0)
    arc_mask = set_ends((jax.random.randint(seeds[1], (ROWS // BLK, COLS // BLK), 0, 4) < 3).astype(jnp.int32), jax.random.fold_in(seeds[1], 1), 0, 1)
    panel_owner = draw_panel_owner(jax.random.fold_in(seeds[3], 71), 0)
    return {"observations": observations, "arc_mask": arc_mask, "panel_owner": panel_owner}


def inner_high(left, right):
    return lax.dot_general(left, right, (((0,), (0,)), ((), ())), precision=lax.Precision.HIGHEST, preferred_element_type=left.dtype)

def matmul_high(left, right):
    return jnp.dot(left, right, precision=lax.Precision.HIGHEST, preferred_element_type=left.dtype)

def expand_mask(observations, arc_mask):
    row_blocks, col_blocks = arc_mask.shape
    shaped = observations.reshape(row_blocks, BLK, col_blocks, BLK)
    masked = shaped * arc_mask.astype(observations.dtype)[:, None, :, None]
    return masked.reshape(observations.shape) / math.sqrt(ROWS)

def reference(observations, arc_mask, panel_owner):
    design = expand_mask(observations, arc_mask)
    rows_out = []
    for panel_turn in range(2):
        col_start = (panel_owner[panel_turn] * PANEL).astype(jnp.int32)
        panel_cols = lax.dynamic_slice_in_dim(design, col_start, PANEL, 1)
        gram_block = inner_high(panel_cols, panel_cols)
        cross_sums = inner_high(panel_cols, design)
        chol_lower = jnp.linalg.cholesky(gram_block)
        factor = jax.scipy.linalg.solve_triangular(chol_lower, cross_sums, lower=True)
        rows_out.append(factor)
        if panel_turn == 0:
            coefficients = jax.scipy.linalg.solve_triangular(chol_lower.T, factor, lower=False)
            design = design - matmul_high(panel_cols, coefficients)
    return jnp.concatenate(rows_out, 0)
```

```python
import math

import jax
import jax.numpy as jnp
from jax import lax
from jax.experimental import pallas as pl
from jax.experimental.pallas import tpu as pltpu
from jax.sharding import PartitionSpec as P

PANEL = 256
BLK = 128
TILE = 128
HIGHEST = lax.Precision.HIGHEST


def dot_nt(left, right):
    return lax.dot_general(
        left, right, (((1,), (1,)), ((), ())), precision=HIGHEST, preferred_element_type=jnp.float32
    )


def dot_tn(left, right):
    return lax.dot_general(
        left, right, (((0,), (0,)), ((), ())), precision=HIGHEST, preferred_element_type=jnp.float32
    )


def dot_nn(left, right):
    return jnp.dot(left, right, precision=HIGHEST, preferred_element_type=jnp.float32)


def tile_inverse(tile, width=8):
    shape = (8, TILE)
    lanes = lax.broadcasted_iota(jnp.int32, shape, 1)
    subl = lax.broadcasted_iota(jnp.int32, shape, 0)
    count = TILE // 8
    rows = [tile[8 * i:8 * i + 8, :] for i in range(count)]
    for start in range(0, TILE, width):
        base = start // 8
        cols = [
            {i: jnp.broadcast_to(rows[i][:, start + c:start + c + 1], shape) for i in range(base, count)}
            for c in range(width)
        ]
        for c in range(width):
            col = start + c
            sub = col % 8
            pivot = jnp.broadcast_to(cols[c][base][sub:sub + 1, :], shape)
            inv = 1.0 / pivot
            prow = jnp.broadcast_to(rows[base][sub:sub + 1, :], shape) * inv
            prow = jnp.where(lanes == col, inv, prow)
            coef = {
                d: jnp.broadcast_to(cols[d][base][sub:sub + 1, :], shape) * inv for d in range(c + 1, width)
            }
            for i in range(base, count):
                if i == base and sub == 7:
                    continue
                mult = cols[c][i]
                keep = lanes == col
                if i == base:
                    mult = jnp.where(subl > sub, mult, 0.0)
                    keep = keep & (subl > sub)
                for d in range(c + 1, width):
                    cols[d][i] = cols[d][i] - mult * coef[d]
                rows[i] = jnp.where(keep, 0.0, rows[i]) - mult * prow
            rows[base] = jnp.where((lanes == col) & (subl == sub), pivot, rows[base])
    out = []
    for i in range(count):
        on_diag = lanes == subl + 8 * i
        diag = jnp.sum(jnp.where(on_diag, rows[i], 0.0), axis=1, keepdims=True)
        scaled = jnp.where(on_diag, 1.0, rows[i]) * lax.rsqrt(diag)
        out.append(jnp.where(lanes <= subl + 8 * i, scaled, 0.0))
    return jnp.concatenate(out, 0)


def factor_inverse(ref, order):
    count = order // TILE
    for k in range(count):
        low, top = k * TILE, (k + 1) * TILE
        inv = tile_inverse(ref[low:top, low:top])
        ref[low:top, low:top] = inv
        if k:
            ref[low:top, :low] = dot_nn(inv, ref[low:top, :low])
        if k + 1 < count:
            below = dot_nt(ref[top:, low:top], inv)
            for i in range(k + 1, count):
                part = below[(i - k - 1) * TILE:(i - k) * TILE]
                ref[i * TILE:(i + 1) * TILE, top:(i + 1) * TILE] -= dot_nt(part, below[:(i - k) * TILE])
            if k:
                ref[top:, :low] -= dot_nn(below, ref[low:top, :low])
            ref[top:, low:top] = -dot_nn(below, inv)
    for i in range(count - 1):
        ref[i * TILE:(i + 1) * TILE, (i + 1) * TILE:] = jnp.zeros((TILE, order - (i + 1) * TILE), jnp.float32)


def factor_kernel(gram_ref, out_ref):
    out_ref[...] = gram_ref[...]
    factor_inverse(out_ref, gram_ref.shape[0])


def factor_call(gram):
    return pl.pallas_call(
        factor_kernel,
        out_shape=jax.ShapeDtypeStruct(gram.shape, jnp.float32),
        compiler_params=pltpu.CompilerParams(vmem_limit_bytes=32 << 20),
        name="factor",
    )(gram)


def shards(observations, arc_mask, panel_owner):
    row_count, col_count = observations.shape
    row_blocks, col_blocks = arc_mask.shape
    total_rows = row_count * lax.axis_size("arc")
    shaped = observations.reshape(row_blocks, BLK, col_blocks, BLK)
    masked = shaped * arc_mask.astype(jnp.float32)[:, None, :, None]
    design = masked.reshape(row_count, col_count) / math.sqrt(total_rows)
    here = lax.axis_index("par")
    parts = []
    for turn in range(2):
        start = panel_owner[turn] * PANEL
        root = start // col_count
        local = lax.dynamic_slice_in_dim(design, start - root * col_count, PANEL, 1)
        parts.append(jnp.where(here == root, local, jnp.zeros_like(local)))
    panels = lax.psum(jnp.concatenate(parts, 1), "par")
    gram = lax.psum(dot_tn(panels, panels), "arc")
    weights = dot_nt(factor_call(gram), panels)
    return lax.psum_scatter(dot_nn(weights, design), "arc", scatter_dimension=0, tiled=True)


def solution(mesh):
    return jax.shard_map(
        shards,
        mesh=mesh,
        in_specs=(P("arc", "par"), P("arc", "par"), P()),
        out_specs=P("arc", "par"),
        check_vma=False,
    )
```

```python
import functools
import math

import jax
import jax.numpy as jnp
from jax import lax
from jax.experimental import pallas as pl
from jax.experimental.pallas import tpu as pltpu
from jax.sharding import PartitionSpec as P

PANEL = 256
BLK = 128
TILE = 128
HIGHEST = lax.Precision.HIGHEST
MESH = pl.DeviceIdType.MESH
F32 = jnp.float32
BF16 = jnp.bfloat16


def dot_nt(left, right):
    return lax.dot_general(left, right, (((1,), (1,)), ((), ())), precision=HIGHEST, preferred_element_type=F32)


def dot_nn(left, right):
    return jnp.dot(left, right, precision=HIGHEST, preferred_element_type=F32)


def halves(value):
    high = value.astype(BF16)
    return high, (value - high.astype(F32)).astype(BF16)


def tile_inverse(tile, width=8):
    lanes = lax.broadcasted_iota(jnp.int32, (8, TILE), 1)
    subl = lax.broadcasted_iota(jnp.int32, (8, TILE), 0)
    zero = jnp.zeros((8, TILE), F32)
    done = []
    tail = tile
    for start in range(0, TILE, width):
        base = start // 8
        size = TILE - 8 * base - 8
        head, tail = tail[:8], tail[8:]
        tail_lanes = lax.broadcasted_iota(jnp.int32, (size, TILE), 1) if size else None
        head_cols = [jnp.broadcast_to(head[:, start + c:start + c + 1], (8, TILE)) for c in range(width)]
        tail_cols = [jnp.broadcast_to(tail[:, start + c:start + c + 1], (size, TILE)) for c in range(width)] if size else None
        for c in range(width):
            col = start + c
            pivot = jnp.broadcast_to(head_cols[c][c:c + 1, :], (8, TILE))
            inv = 1.0 / pivot
            on_col = lanes == col
            prow = jnp.where(on_col, inv, jnp.broadcast_to(head[c:c + 1, :], (8, TILE)) * inv)
            below = subl > c
            mult = jnp.where(below, head_cols[c], zero)
            coefs = [jnp.broadcast_to(head_cols[d][c:c + 1, :], (8, TILE)) * inv for d in range(c + 1, width)]
            for d in range(c + 1, width):
                head_cols[d] = head_cols[d] - mult * coefs[d - c - 1]
            head = jnp.where(on_col, jnp.where(below, zero, jnp.where(subl == c, pivot, head)), head) - mult * prow
            if size:
                for d in range(c + 1, width):
                    tail_cols[d] = tail_cols[d] - tail_cols[c] * jnp.broadcast_to(coefs[d - c - 1][:1], (size, TILE))
                tail = jnp.where(tail_lanes == col, 0.0, tail) - tail_cols[c] * jnp.broadcast_to(prow[:1], (size, TILE))
        on_diag = lanes == subl + start
        diag = jnp.sum(jnp.where(on_diag, head, zero), axis=1, keepdims=True)
        scaled = jnp.where(on_diag, 1.0, head) * lax.rsqrt(diag)
        done.append(jnp.where(lanes <= subl + start, scaled, zero))
    return jnp.concatenate(done, 0)


def factor_step(ref, k, count):
    low, top = k * TILE, (k + 1) * TILE
    inv = tile_inverse(ref[low:top, low:top])
    ref[low:top, low:top] = inv
    if k:
        ref[low:top, :low] = dot_nn(inv, ref[low:top, :low])
    if k + 1 < count:
        below = dot_nt(ref[top:, low:top], inv)
        for i in range(k + 1, count):
            part = below[(i - k - 1) * TILE:(i - k) * TILE]
            ref[i * TILE:(i + 1) * TILE, top:(i + 1) * TILE] -= dot_nt(part, below[:(i - k) * TILE])
        if k:
            ref[top:, :low] -= dot_nn(below, ref[low:top, :low])
        ref[top:, low:top] = -dot_nn(below, inv)


def kernel(
    n_arc, n_par,
    obs_ref, mask_ref, owner_ref, out_ref,
    part_ref, piece_ref, panel_ref, stack_ref,
    gram_ref, gram_piece_ref, gram_all_ref, fac_ref,
    to_core_ref, from_core_ref, sums_ref, from_one_ref, from_two_ref, result_ref,
    part_sems, panel_sems, gram_sems, all_sems, fwd_sems, core_sems, one_sems, two_sems, out_sems,
):
    rows, cols = obs_ref.shape
    order = 2 * PANEL
    share = rows // n_par
    slice_rows = gram_piece_ref.shape[1]
    width = cols // 16
    out_rows = out_ref.shape[0]
    tiles = order // TILE
    chips = n_arc // 2
    scale = 1.0 / math.sqrt(rows * n_arc)
    arc = lax.axis_index("arc")
    par = lax.axis_index("par")
    chip = arc // 2
    core = arc % 2

    def send(src, dst, sems, slot, target):
        return pltpu.make_async_remote_copy(
            src_ref=src, dst_ref=dst, send_sem=sems.at[0, slot], recv_sem=sems.at[1, slot],
            device_id=target, device_id_type=MESH,
        )

    def each(count, body):
        lax.fori_loop(0, count, lambda i, carry: (body(i), carry)[1], 0)

    def par_peer(i):
        return lax.rem(par + i + 1, n_par)

    def arc_peer(i):
        return lax.rem(arc + i + 1, n_arc)

    barrier = pltpu.get_barrier_semaphore()
    each(n_par - 1, lambda i: pl.semaphore_signal(barrier, inc=1, device_id={"par": par_peer(i)}, device_id_type=MESH))
    each(n_arc - 1, lambda i: pl.semaphore_signal(barrier, inc=1, device_id={"arc": arc_peer(i)}, device_id_type=MESH))

    held = cols // PANEL
    for turn in range(2):
        chosen = [jnp.where(owner_ref[turn] == par * held + b, 1.0, 0.0) for b in range(held)]
        for half in range(PANEL // BLK):
            for band in range(rows // BLK):
                low, top = band * BLK, (band + 1) * BLK
                total = jnp.zeros((BLK, BLK), F32)
                for b in range(held):
                    block = b * (PANEL // BLK) + half
                    weight = mask_ref[band, block].astype(F32) * chosen[b]
                    total = total + obs_ref[low:top, block * BLK:(block + 1) * BLK] * weight
                at = turn * PANEL + half * BLK
                part_ref[low:top, at:at + BLK] = total

    pl.semaphore_wait(barrier, n_par + n_arc - 2)

    def part_copy(i):
        peer = par_peer(i)
        src = part_ref.at[pl.ds(pl.multiple_of(peer * share, 8), share)]
        return send(src, piece_ref.at[i], part_sems, i, {"par": peer})

    each(n_par - 1, lambda i: part_copy(i).start())
    each(n_par - 1, lambda i: part_copy(i).wait_recv())
    own_share = pl.ds(pl.multiple_of(par * share, 8), share)
    total = part_ref[own_share, :]
    for i in range(n_par - 1):
        total = total + piece_ref[i]
    panel_ref[own_share, :] = total

    def panel_copy(i):
        return send(panel_ref.at[own_share], panel_ref.at[own_share], panel_sems, i, {"par": par_peer(i)})

    each(n_par - 1, lambda i: panel_copy(i).start())
    each(n_par - 1, lambda i: panel_copy(i).wait_recv())

    panel = panel_ref[...]
    turned = panel.T
    for i in range(tiles):
        gram_rows = dot_nn(turned[i * TILE:(i + 1) * TILE], panel[:, :(i + 1) * TILE])
        for j in range(i + 1):
            at = (i * (i + 1) // 2 + j) * TILE
            gram_ref[at:at + TILE, :] = gram_rows[:, j * TILE:(j + 1) * TILE]

    def gram_copy(i):
        peer = arc_peer(i)
        at = pl.multiple_of((2 * par + peer % 2) * slice_rows, 8)
        return send(gram_ref.at[pl.ds(at, slice_rows)], gram_piece_ref.at[i], gram_sems, i, {"arc": peer})

    each(n_arc - 1, lambda i: gram_copy(i).start())

    high, low = halves(turned)
    stack_ref[...] = jnp.concatenate([high, high, low], 1)

    def owner_chip(t):
        side = t % 2
        across = chips - 1 - chip
        beside = chip + 1 - 2 * (chip % 2)
        return [
            (lax.rem(chip + 2, chips), lax.rem(chip + 2, chips)),
            (beside, across),
            (across, beside),
            (chip, chip),
        ][t // 2][side]

    def column_of(half, t):
        return pl.multiple_of((half * 8 + (t % 2) * 4 + owner_chip(t)) * width, BLK)

    def cross_tile(half, t):
        column = column_of(half, t)
        bands = []
        for band in range(rows // BLK):
            parts = [
                obs_ref[band * BLK:(band + 1) * BLK, pl.ds(pl.multiple_of(column + h * BLK, BLK), BLK)]
                * mask_ref[band, column // BLK + h].astype(F32)
                for h in range(width // BLK)
            ]
            bands.append(jnp.concatenate(parts, 1))
        up, down = halves(jnp.concatenate(bands, 0))
        return jnp.dot(stack_ref[...], jnp.concatenate([up, down, up], 0), preferred_element_type=F32)

    def core_copy(t):
        return send(to_core_ref.at[t], from_core_ref.at[t], core_sems, t, {"arc": arc + 1 - 2 * core})

    for t in range(8):
        to_core_ref[t] = cross_tile(1 - core, t)
        core_copy(t).start()

    each(n_arc - 1, lambda i: gram_copy(i).wait_recv())
    own_at = pl.multiple_of((2 * par + core) * slice_rows, 8)
    gram_total = gram_ref[pl.ds(own_at, slice_rows), :]
    for i in range(n_arc - 1):
        gram_total = gram_total + gram_piece_ref[i]
    gram_all_ref[par, core] = gram_total

    def all_copy(i):
        here = gram_all_ref.at[par, core]
        return send(here, here, all_sems, i, {"par": par_peer(i)})

    each(n_par - 1, lambda i: all_copy(i).start())

    def one_copy(t):
        to = (chip + 1 - 2 * (chip % 2)) if t % 2 == 0 else (chips - 1 - chip)
        return send(sums_ref.at[t], from_one_ref.at[t], one_sems, t, {"arc": 2 * to + core})

    for t in range(8):
        own = cross_tile(core, t)
        core_copy(t).wait_recv()
        sums_ref[t] = own + from_core_ref[t]
        if t < 4:
            one_copy(t).start()

    each(n_par - 1, lambda i: all_copy(i).wait_recv())
    fwd = send(gram_all_ref.at[:, core], gram_all_ref.at[:, core], fwd_sems, 0, {"arc": arc + 1 - 2 * core})
    fwd.start()
    fwd.wait_recv()
    flat = gram_all_ref[...].reshape(2 * n_par * slice_rows, TILE)
    for i in range(tiles):
        for j in range(i + 1):
            at = (i * (i + 1) // 2 + j) * TILE
            fac_ref[i * TILE:(i + 1) * TILE, j * TILE:(j + 1) * TILE] = flat[at:at + TILE]
        if i + 1 < tiles:
            fac_ref[i * TILE:(i + 1) * TILE, (i + 1) * TILE:] = jnp.zeros((TILE, order - (i + 1) * TILE), F32)

    def two_copy(t):
        to = (chips - 1 - chip) if t % 2 == 0 else (chip + 1 - 2 * (chip % 2))
        return send(sums_ref.at[4 + t], from_two_ref.at[t], two_sems, t, {"arc": 2 * to + core})

    for k in range(tiles):
        factor_step(fac_ref, k, tiles)
        if k == 1:
            for t in range(2):
                one_copy(t).wait_recv()
                sums_ref[4 + t] = sums_ref[4 + t] + from_one_ref[t]
                two_copy(t).start()

    def out_copy(t, i):
        peer = arc_peer(i)
        src = result_ref.at[t, pl.ds(pl.multiple_of(peer * out_rows, 8), out_rows)]
        dst = out_ref.at[:, pl.ds(column_of(core, 6 + t), width)]
        return send(src, dst, out_sems, t * (n_arc - 1) + i, {"arc": peer})

    for t in range(2):
        one_copy(2 + t).wait_recv()
        two_copy(t).wait_recv()
        whole = sums_ref[6 + t] + from_one_ref[2 + t] + from_two_ref[t]
        for i in range(tiles):
            depth = (i + 1) * TILE
            result_ref[t, i * TILE:depth] = dot_nn(fac_ref[i * TILE:depth, :depth], whole[:depth]) * scale
        each(n_arc - 1, lambda i: out_copy(t, i).start())
        out_ref[:, pl.ds(column_of(core, 6 + t), width)] = result_ref[
            t, pl.ds(pl.multiple_of(arc * out_rows, 8), out_rows)
        ]

    each(n_par - 1, lambda i: part_copy(i).wait_send())
    each(n_par - 1, lambda i: panel_copy(i).wait_send())
    each(n_arc - 1, lambda i: gram_copy(i).wait_send())
    each(n_par - 1, lambda i: all_copy(i).wait_send())
    fwd.wait_send()
    for t in range(8):
        core_copy(t).wait_send()
    for t in range(4):
        one_copy(t).wait_send()
    for t in range(2):
        two_copy(t).wait_send()
    for t in range(2):
        each(n_arc - 1, lambda i: out_copy(t, i).wait())


def shards(observations, arc_mask, panel_owner):
    n_arc, n_par = lax.axis_size("arc"), lax.axis_size("par")
    rows, cols = observations.shape
    order = 2 * PANEL
    share = rows // n_par
    width = cols // 16
    tiles = order // TILE
    slice_rows = tiles * (tiles + 1) // 2 * TILE // (2 * n_par)

    def pair(count):
        return pltpu.SemaphoreType.DMA((2, count))

    return pl.pallas_call(
        functools.partial(kernel, n_arc, n_par),
        out_shape=jax.ShapeDtypeStruct((order // n_arc, cols), F32),
        in_specs=[
            pl.BlockSpec(memory_space=pltpu.VMEM),
            pl.BlockSpec(memory_space=pltpu.SMEM),
            pl.BlockSpec(memory_space=pltpu.SMEM),
        ],
        out_specs=pl.BlockSpec(memory_space=pltpu.VMEM),
        scratch_shapes=[
            pltpu.VMEM((rows, order), F32),
            pltpu.VMEM((n_par - 1, share, order), F32),
            pltpu.VMEM((rows, order), F32),
            pltpu.VMEM((order, 3 * rows), BF16),
            pltpu.VMEM((2 * n_par * slice_rows, TILE), F32),
            pltpu.VMEM((n_arc - 1, slice_rows, TILE), F32),
            pltpu.VMEM((n_par, 2, slice_rows, TILE), F32),
            pltpu.VMEM((order, order), F32),
            pltpu.VMEM((8, order, width), F32),
            pltpu.VMEM((8, order, width), F32),
            pltpu.VMEM((8, order, width), F32),
            pltpu.VMEM((4, order, width), F32),
            pltpu.VMEM((2, order, width), F32),
            pltpu.VMEM((2, order, width), F32),
            pair(n_par - 1),
            pair(n_par - 1),
            pair(n_arc - 1),
            pair(n_par - 1),
            pair(1),
            pair(8),
            pair(4),
            pair(2),
            pair(2 * (n_arc - 1)),
        ],
        compiler_params=pltpu.CompilerParams(
            collective_id=0, has_side_effects=True, vmem_limit_bytes=48 << 20
        ),
        name="info_rows",
    )(observations, arc_mask, panel_owner)


def solution(mesh):
    return jax.shard_map(
        shards,
        mesh=mesh,
        in_specs=(P("arc", "par"), P("arc", "par"), P()),
        out_specs=P("arc", "par"),
        check_vma=False,
    )
```

```python
import functools
import math

import jax
import jax.numpy as jnp
from jax import lax
from jax.experimental import pallas as pl
from jax.experimental.pallas import tpu as pltpu
from jax.sharding import PartitionSpec as P

PANEL = 256
BLK = 128
TILE = 128
HIGHEST = lax.Precision.HIGHEST
MESH = pl.DeviceIdType.MESH
F32 = jnp.float32
BF16 = jnp.bfloat16


def dot_nt(left, right):
    return lax.dot_general(left, right, (((1,), (1,)), ((), ())), precision=HIGHEST, preferred_element_type=F32)


def dot_nn(left, right):
    return jnp.dot(left, right, precision=HIGHEST, preferred_element_type=F32)


def halves(value):
    high = value.astype(BF16)
    return high, (value - high.astype(F32)).astype(BF16)


def tile_inverse(tile, width=8):
    lanes = lax.broadcasted_iota(jnp.int32, (8, TILE), 1)
    subl = lax.broadcasted_iota(jnp.int32, (8, TILE), 0)
    zero = jnp.zeros((8, TILE), F32)
    done = []
    tail = tile
    for start in range(0, TILE, width):
        base = start // 8
        size = TILE - 8 * base - 8
        head, tail = tail[:8], tail[8:]
        tail_lanes = lax.broadcasted_iota(jnp.int32, (size, TILE), 1) if size else None
        head_cols = [jnp.broadcast_to(head[:, start + c:start + c + 1], (8, TILE)) for c in range(width)]
        tail_cols = [jnp.broadcast_to(tail[:, start + c:start + c + 1], (size, TILE)) for c in range(width)] if size else None
        for c in range(width):
            col = start + c
            pivot = jnp.broadcast_to(head_cols[c][c:c + 1, :], (8, TILE))
            inv = 1.0 / pivot
            on_col = lanes == col
            prow = jnp.where(on_col, inv, jnp.broadcast_to(head[c:c + 1, :], (8, TILE)) * inv)
            below = subl > c
            mult = jnp.where(below, head_cols[c], zero)
            coefs = [jnp.broadcast_to(head_cols[d][c:c + 1, :], (8, TILE)) * inv for d in range(c + 1, width)]
            for d in range(c + 1, width):
                head_cols[d] = head_cols[d] - mult * coefs[d - c - 1]
            head = jnp.where(on_col, jnp.where(below, zero, jnp.where(subl == c, pivot, head)), head) - mult * prow
            if size:
                for d in range(c + 1, width):
                    tail_cols[d] = tail_cols[d] - tail_cols[c] * jnp.broadcast_to(coefs[d - c - 1][:1], (size, TILE))
                tail = jnp.where(tail_lanes == col, 0.0, tail) - tail_cols[c] * jnp.broadcast_to(prow[:1], (size, TILE))
        on_diag = lanes == subl + start
        diag = jnp.sum(jnp.where(on_diag, head, zero), axis=1, keepdims=True)
        scaled = jnp.where(on_diag, 1.0, head) * lax.rsqrt(diag)
        done.append(jnp.where(lanes <= subl + start, scaled, zero))
    return jnp.concatenate(done, 0)


def factor_step(ref, k, count):
    low, top = k * TILE, (k + 1) * TILE
    inv = tile_inverse(ref[low:top, low:top])
    ref[low:top, low:top] = inv
    if k:
        ref[low:top, :low] = dot_nn(inv, ref[low:top, :low])
    if k + 1 < count:
        below = dot_nt(ref[top:, low:top], inv)
        for i in range(k + 1, count):
            part = below[(i - k - 1) * TILE:(i - k) * TILE]
            ref[i * TILE:(i + 1) * TILE, top:(i + 1) * TILE] -= dot_nt(part, below[:(i - k) * TILE])
        if k:
            ref[top:, :low] -= dot_nn(below, ref[low:top, :low])
        ref[top:, low:top] = -dot_nn(below, inv)


def kernel(
    n_arc, n_par,
    obs_hbm, mask_hbm, owner_hbm, out_ref,
    obs_ref, mask_ref, owner_ref,
    part_ref, piece_ref, panel_ref, other_obs_ref, other_panel_ref, stack_ref,
    gram_ref, gram_piece_ref, gram_all_ref, fac_ref,
    sums_ref, from_one_ref, from_two_ref, result_ref,
    load_sems, part_sems, last_sems, panel_sems, gram_sems, all_sems, core_sems, one_sems, two_sems, out_sems,
):
    rows, cols = obs_ref.shape
    order = 2 * PANEL
    share = rows // n_par
    slice_rows = gram_piece_ref.shape[1]
    width = cols // 16
    out_rows = out_ref.shape[0]
    tiles = order // TILE
    chips = n_arc // 2
    scale = 1.0 / math.sqrt(rows * n_arc)
    arc = lax.axis_index("arc")
    par = lax.axis_index("par")
    chip = arc // 2
    core = arc % 2

    def send(src, dst, sems, slot, target):
        return pltpu.make_async_remote_copy(
            src_ref=src, dst_ref=dst, send_sem=sems.at[0, slot], recv_sem=sems.at[1, slot],
            device_id=target, device_id_type=MESH,
        )

    def each(count, body):
        lax.fori_loop(0, count, lambda i, carry: (body(i), carry)[1], 0)

    def par_peer(i):
        return lax.rem(par + i + 1, n_par)

    def arc_peer(i):
        return lax.rem(arc + i + 1, n_arc)

    sibling = {"arc": arc + 1 - 2 * core}
    loads = [
        pltpu.make_async_copy(src, dst, load_sems.at[i])
        for i, (src, dst) in enumerate([(mask_hbm, mask_ref), (owner_hbm, owner_ref), (obs_hbm, obs_ref)])
    ]
    for load in loads:
        load.start()

    barrier = pltpu.get_barrier_semaphore()
    each(n_par - 1, lambda i: pl.semaphore_signal(barrier, inc=1, device_id={"par": par_peer(i)}, device_id_type=MESH))
    each(n_arc - 1, lambda i: pl.semaphore_signal(barrier, inc=1, device_id={"arc": arc_peer(i)}, device_id_type=MESH))
    for load in loads:
        load.wait()

    held = cols // PANEL
    last = n_par * held - 1
    last_first = owner_ref[0] == last
    other = jnp.where(last_first, owner_ref[1], owner_ref[0])
    chosen = [jnp.where(other == par * held + b, 1.0, 0.0) for b in range(held)]
    for half in range(PANEL // BLK):
        for band in range(rows // BLK):
            low, top = band * BLK, (band + 1) * BLK
            total = jnp.zeros((BLK, BLK), F32)
            for b in range(held):
                block = b * (PANEL // BLK) + half
                left, right = block * BLK, (block + 1) * BLK
                masked = obs_ref[low:top, left:right] * mask_ref[band, block].astype(F32)
                obs_ref[low:top, left:right] = masked
                total = total + masked * chosen[b]
            part_ref[low:top, half * BLK:(half + 1) * BLK] = total

    pl.semaphore_wait(barrier, n_par + n_arc - 2)

    def share_of(device):
        return pl.ds(pl.multiple_of(device * share, 8), share)

    def part_copy(i):
        peer = par_peer(i)
        return send(part_ref.at[share_of(peer)], piece_ref.at[i], part_sems, i, {"par": peer})

    def last_copy(i):
        peer = par_peer(i)
        return send(
            obs_ref.at[share_of(peer), cols - PANEL:], panel_ref.at[share_of(peer), PANEL:], last_sems, peer, {"par": peer}
        )

    def last_arrival():
        here = panel_ref.at[share_of(par), PANEL:]
        return send(here, here, last_sems, par, {"par": n_par - 1})

    def obs_copy():
        there = pl.ds(pl.multiple_of((1 - core) * (cols // 2), BLK), cols // 2)
        return send(obs_ref.at[:, there], other_obs_ref, core_sems, 0, sibling)

    def sibling_panel_copy():
        return send(panel_ref, other_panel_ref, core_sems, 1, sibling)

    owns_last = par == n_par - 1
    own_share = share_of(par)

    @pl.when(owns_last)
    def _():
        each(n_par - 1, lambda i: last_copy(i).start())
        panel_ref[own_share, PANEL:] = obs_ref[own_share, cols - PANEL:]

    each(n_par - 1, lambda i: part_copy(i).start())
    obs_copy().start()
    each(n_par - 1, lambda i: part_copy(i).wait_recv())
    total = part_ref[own_share, :]
    for i in range(n_par - 1):
        total = total + piece_ref[i]
    panel_ref[own_share, :PANEL] = total

    @pl.when(jnp.logical_not(owns_last))
    def _():
        last_arrival().wait_recv()

    def panel_copy(i):
        return send(panel_ref.at[own_share], panel_ref.at[own_share], panel_sems, i, {"par": par_peer(i)})

    each(n_par - 1, lambda i: panel_copy(i).start())
    each(n_par - 1, lambda i: panel_copy(i).wait_recv())
    sibling_panel_copy().start()

    def in_order(ref):
        one, two = ref[:, :PANEL], ref[:, PANEL:]
        return jnp.concatenate([jnp.where(last_first, two, one), jnp.where(last_first, one, two)], 1)

    panel = in_order(panel_ref)
    turned = panel.T
    for i in range(tiles):
        gram_rows = dot_nn(turned[i * TILE:(i + 1) * TILE], panel[:, :(i + 1) * TILE])
        for j in range(i + 1):
            at = (i * (i + 1) // 2 + j) * TILE
            gram_ref[at:at + TILE, :] = gram_rows[:, j * TILE:(j + 1) * TILE]

    def gram_copy(i):
        peer = arc_peer(i)
        at = pl.multiple_of((2 * par + peer % 2) * slice_rows, 8)
        return send(gram_ref.at[pl.ds(at, slice_rows)], gram_piece_ref.at[i], gram_sems, i, {"arc": peer})

    each(n_arc - 1, lambda i: gram_copy(i).start())

    def fill_stack(at, turned_panel):
        high, low = halves(turned_panel)
        stack_ref[:, at:at + 3 * rows] = jnp.concatenate([high, high, low], 1)

    fill_stack(0, turned)
    sibling_panel_copy().wait_recv()
    fill_stack(3 * rows, in_order(other_panel_ref).T)

    def owner_chip(t):
        side = t % 2
        across = chips - 1 - chip
        beside = chip + 1 - 2 * (chip % 2)
        return [
            (lax.rem(chip + 2, chips), lax.rem(chip + 2, chips)),
            (beside, across),
            (across, beside),
            (chip, chip),
        ][t // 2][side]

    def column_of(t):
        return pl.multiple_of(((t % 2) * 4 + owner_chip(t)) * width, BLK)

    def cross_tile(t):
        own = obs_ref[:, pl.ds(pl.multiple_of(core * (cols // 2) + column_of(t), BLK), width)]
        theirs = other_obs_ref[:, pl.ds(column_of(t), width)]
        up, down = halves(own)
        their_up, their_down = halves(theirs)
        stacked = jnp.concatenate([up, down, up, their_up, their_down, their_up], 0)
        return jnp.dot(stack_ref[...], stacked, preferred_element_type=F32)

    def one_copy(t):
        to = (chip + 1 - 2 * (chip % 2)) if t % 2 == 0 else (chips - 1 - chip)
        return send(sums_ref.at[t], from_one_ref.at[t], one_sems, t, {"arc": 2 * to + core})

    obs_copy().wait_recv()
    for t in range(4):
        sums_ref[t] = cross_tile(t)
        one_copy(t).start()

    each(n_arc - 1, lambda i: gram_copy(i).wait_recv())
    own_at = pl.multiple_of((2 * par + core) * slice_rows, 8)
    gram_total = gram_ref[pl.ds(own_at, slice_rows), :]
    for i in range(n_arc - 1):
        gram_total = gram_total + gram_piece_ref[i]
    gram_all_ref[par, core] = gram_total

    def all_copy(i):
        here = gram_all_ref.at[par, core]
        return send(here, here, all_sems, i, {"par": par_peer(i)})

    each(n_par - 1, lambda i: all_copy(i).start())

    for t in range(4, 8):
        sums_ref[t] = cross_tile(t)

    each(n_par - 1, lambda i: all_copy(i).wait_recv())
    fwd = send(gram_all_ref.at[:, core], gram_all_ref.at[:, core], core_sems, 2, sibling)
    fwd.start()
    fwd.wait_recv()
    flat = gram_all_ref[...].reshape(2 * n_par * slice_rows, TILE)
    for i in range(tiles):
        for j in range(i + 1):
            at = (i * (i + 1) // 2 + j) * TILE
            fac_ref[i * TILE:(i + 1) * TILE, j * TILE:(j + 1) * TILE] = flat[at:at + TILE]
        if i + 1 < tiles:
            fac_ref[i * TILE:(i + 1) * TILE, (i + 1) * TILE:] = jnp.zeros((TILE, order - (i + 1) * TILE), F32)

    def two_copy(t):
        to = (chips - 1 - chip) if t % 2 == 0 else (chip + 1 - 2 * (chip % 2))
        return send(sums_ref.at[4 + t], from_two_ref.at[t], two_sems, t, {"arc": 2 * to + core})

    for k in range(tiles):
        factor_step(fac_ref, k, tiles)
        if k == 1:
            for t in range(2):
                one_copy(t).wait_recv()
                sums_ref[4 + t] = sums_ref[4 + t] + from_one_ref[t]
                two_copy(t).start()

    def out_column(t):
        return pl.multiple_of(core * (cols // 2) + column_of(6 + t), BLK)

    def out_copy(t, i):
        peer = arc_peer(i)
        src = result_ref.at[t, pl.ds(pl.multiple_of(peer * out_rows, 8), out_rows)]
        dst = out_ref.at[:, pl.ds(out_column(t), width)]
        return send(src, dst, out_sems, t * (n_arc - 1) + i, {"arc": peer})

    for t in range(2):
        one_copy(2 + t).wait_recv()
        two_copy(t).wait_recv()
        whole = sums_ref[6 + t] + from_one_ref[2 + t] + from_two_ref[t]
        for i in range(tiles):
            depth = (i + 1) * TILE
            result_ref[t, i * TILE:depth] = dot_nn(fac_ref[i * TILE:depth, :depth], whole[:depth]) * scale
        each(n_arc - 1, lambda i: out_copy(t, i).start())
        out_ref[:, pl.ds(out_column(t), width)] = result_ref[
            t, pl.ds(pl.multiple_of(arc * out_rows, 8), out_rows)
        ]

    each(n_par - 1, lambda i: part_copy(i).wait_send())
    each(n_par - 1, lambda i: panel_copy(i).wait_send())
    each(n_arc - 1, lambda i: gram_copy(i).wait_send())
    each(n_par - 1, lambda i: all_copy(i).wait_send())
    fwd.wait_send()
    obs_copy().wait_send()
    sibling_panel_copy().wait_send()

    @pl.when(owns_last)
    def _():
        each(n_par - 1, lambda i: last_copy(i).wait_send())

    for t in range(4):
        one_copy(t).wait_send()
    for t in range(2):
        two_copy(t).wait_send()
    for t in range(2):
        each(n_arc - 1, lambda i: out_copy(t, i).wait())


def shards(observations, arc_mask, panel_owner):
    n_arc, n_par = lax.axis_size("arc"), lax.axis_size("par")
    rows, cols = observations.shape
    order = 2 * PANEL
    share = rows // n_par
    width = cols // 16
    tiles = order // TILE
    slice_rows = tiles * (tiles + 1) // 2 * TILE // (2 * n_par)

    def pair(count):
        return pltpu.SemaphoreType.DMA((2, count))

    return pl.pallas_call(
        functools.partial(kernel, n_arc, n_par),
        out_shape=jax.ShapeDtypeStruct((order // n_arc, cols), F32),
        in_specs=[pl.BlockSpec(memory_space=pl.ANY)] * 3,
        out_specs=pl.BlockSpec(memory_space=pltpu.VMEM),
        scratch_shapes=[
            pltpu.VMEM((rows, cols), F32),
            pltpu.SMEM(arc_mask.shape, jnp.int32),
            pltpu.SMEM(panel_owner.shape, jnp.int32),
            pltpu.VMEM((rows, PANEL), F32),
            pltpu.VMEM((n_par - 1, share, PANEL), F32),
            pltpu.VMEM((rows, order), F32),
            pltpu.VMEM((rows, cols // 2), F32),
            pltpu.VMEM((rows, order), F32),
            pltpu.VMEM((order, 6 * rows), BF16),
            pltpu.VMEM((2 * n_par * slice_rows, TILE), F32),
            pltpu.VMEM((n_arc - 1, slice_rows, TILE), F32),
            pltpu.VMEM((n_par, 2, slice_rows, TILE), F32),
            pltpu.VMEM((order, order), F32),
            pltpu.VMEM((8, order, width), F32),
            pltpu.VMEM((4, order, width), F32),
            pltpu.VMEM((2, order, width), F32),
            pltpu.VMEM((2, order, width), F32),
            pltpu.SemaphoreType.DMA((3,)),
            pair(n_par - 1),
            pair(n_par),
            pair(n_par - 1),
            pair(n_arc - 1),
            pair(n_par - 1),
            pair(3),
            pair(4),
            pair(2),
            pair(2 * (n_arc - 1)),
        ],
        compiler_params=pltpu.CompilerParams(
            collective_id=0, has_side_effects=True, vmem_limit_bytes=60 << 20
        ),
        name="info_rows",
    )(observations, arc_mask, panel_owner)


def solution(mesh):
    return jax.shard_map(
        shards,
        mesh=mesh,
        in_specs=(P("arc", "par"), P("arc", "par"), P()),
        out_specs=P("arc", "par"),
        check_vma=False,
    )
```

```python
import functools
import math

import jax
import jax.numpy as jnp
from jax import lax
from jax.experimental import pallas as pl
from jax.experimental.pallas import tpu as pltpu
from jax.sharding import PartitionSpec as P

PANEL = 256
BLK = 128
TILE = 128
HIGHEST = lax.Precision.HIGHEST
MESH = pl.DeviceIdType.MESH
F32 = jnp.float32
BF16 = jnp.bfloat16


def dot_nt(left, right):
    return lax.dot_general(left, right, (((1,), (1,)), ((), ())), precision=HIGHEST, preferred_element_type=F32)


def dot_nn(left, right):
    return jnp.dot(left, right, precision=HIGHEST, preferred_element_type=F32)


def halves(value):
    high = value.astype(BF16)
    return high, (value - high.astype(F32)).astype(BF16)


def tile_inverse(tile, width=8):
    lanes = lax.broadcasted_iota(jnp.int32, (8, TILE), 1)
    subl = lax.broadcasted_iota(jnp.int32, (8, TILE), 0)
    zero = jnp.zeros((8, TILE), F32)
    done = []
    tail = tile
    for start in range(0, TILE, width):
        base = start // 8
        size = TILE - 8 * base - 8
        head, tail = tail[:8], tail[8:]
        tail_lanes = lax.broadcasted_iota(jnp.int32, (size, TILE), 1) if size else None
        head_cols = [jnp.broadcast_to(head[:, start + c:start + c + 1], (8, TILE)) for c in range(width)]
        tail_cols = [jnp.broadcast_to(tail[:, start + c:start + c + 1], (size, TILE)) for c in range(width)] if size else None
        for c in range(width):
            col = start + c
            pivot = jnp.broadcast_to(head_cols[c][c:c + 1, :], (8, TILE))
            inv = 1.0 / pivot
            on_col = lanes == col
            prow = jnp.where(on_col, inv, jnp.broadcast_to(head[c:c + 1, :], (8, TILE)) * inv)
            below = subl > c
            mult = jnp.where(below, head_cols[c], zero)
            coefs = [jnp.broadcast_to(head_cols[d][c:c + 1, :], (8, TILE)) * inv for d in range(c + 1, width)]
            for d in range(c + 1, width):
                head_cols[d] = head_cols[d] - mult * coefs[d - c - 1]
            head = jnp.where(on_col, jnp.where(below, zero, jnp.where(subl == c, pivot, head)), head) - mult * prow
            if size:
                for d in range(c + 1, width):
                    tail_cols[d] = tail_cols[d] - tail_cols[c] * jnp.broadcast_to(coefs[d - c - 1][:1], (size, TILE))
                tail = jnp.where(tail_lanes == col, 0.0, tail) - tail_cols[c] * jnp.broadcast_to(prow[:1], (size, TILE))
        on_diag = lanes == subl + start
        diag = jnp.sum(jnp.where(on_diag, head, zero), axis=1, keepdims=True)
        scaled = jnp.where(on_diag, 1.0, head) * lax.rsqrt(diag)
        done.append(jnp.where(lanes <= subl + start, scaled, zero))
    return jnp.concatenate(done, 0)


def factor_step(ref, k, count):
    low, top = k * TILE, (k + 1) * TILE
    inv = tile_inverse(ref[low:top, low:top])
    ref[low:top, low:top] = inv
    if k:
        ref[low:top, :low] = dot_nn(inv, ref[low:top, :low])
    if k + 1 < count:
        below = dot_nt(ref[top:, low:top], inv)
        for i in range(k + 1, count):
            part = below[(i - k - 1) * TILE:(i - k) * TILE]
            ref[i * TILE:(i + 1) * TILE, top:(i + 1) * TILE] -= dot_nt(part, below[:(i - k) * TILE])
        if k:
            ref[top:, :low] -= dot_nn(below, ref[low:top, :low])
        ref[top:, low:top] = -dot_nn(below, inv)


def kernel(
    n_arc, n_par,
    obs_hbm, mask_hbm, owner_hbm, out_ref,
    obs_ref, mask_ref, owner_ref,
    part_ref, piece_ref, panel_ref, other_obs_ref, other_panel_ref, stack_ref,
    gram_ref, gram_piece_ref, gram_all_ref, fac_ref,
    sums_ref, from_one_ref, from_two_ref, result_ref,
    load_sems, part_sems, panel_sems, gram_sems, all_sems, core_sems, one_sems, two_sems, out_sems,
):
    rows, cols = obs_ref.shape
    order = 2 * PANEL
    share = rows // n_par
    slice_rows = gram_piece_ref.shape[1]
    width = cols // 16
    out_rows = out_ref.shape[0]
    tiles = order // TILE
    chips = n_arc // 2
    scale = 1.0 / math.sqrt(rows * n_arc)
    arc = lax.axis_index("arc")
    par = lax.axis_index("par")
    chip = arc // 2
    core = arc % 2

    def send(src, dst, sems, slot, target):
        return pltpu.make_async_remote_copy(
            src_ref=src, dst_ref=dst, send_sem=sems.at[0, slot], recv_sem=sems.at[1, slot],
            device_id=target, device_id_type=MESH,
        )

    def each(count, body):
        lax.fori_loop(0, count, lambda i, carry: (body(i), carry)[1], 0)

    def par_peer(i):
        return lax.rem(par + i + 1, n_par)

    def arc_peer(i):
        return lax.rem(arc + i + 1, n_arc)

    sibling = {"arc": arc + 1 - 2 * core}
    loads = [
        pltpu.make_async_copy(src, dst, load_sems.at[i])
        for i, (src, dst) in enumerate([(mask_hbm, mask_ref), (owner_hbm, owner_ref), (obs_hbm, obs_ref)])
    ]
    for load in loads:
        load.start()

    barrier = pltpu.get_barrier_semaphore()
    each(n_par - 1, lambda i: pl.semaphore_signal(barrier, inc=1, device_id={"par": par_peer(i)}, device_id_type=MESH))
    each(n_arc - 1, lambda i: pl.semaphore_signal(barrier, inc=1, device_id={"arc": arc_peer(i)}, device_id_type=MESH))
    for load in loads:
        load.wait()

    held = cols // PANEL
    last = n_par * held - 1
    last_first = owner_ref[0] == last
    other = jnp.where(last_first, owner_ref[1], owner_ref[0])
    chosen = [jnp.where(other == par * held + b, 1.0, 0.0) for b in range(held)]
    for half in range(PANEL // BLK):
        for band in range(rows // BLK):
            low, top = band * BLK, (band + 1) * BLK
            total = jnp.zeros((BLK, BLK), F32)
            for b in range(held):
                block = b * (PANEL // BLK) + half
                left, right = block * BLK, (block + 1) * BLK
                masked = obs_ref[low:top, left:right] * mask_ref[band, block].astype(F32)
                obs_ref[low:top, left:right] = masked
                total = total + masked * chosen[b]
            part_ref[low:top, half * BLK:(half + 1) * BLK] = total

    pl.semaphore_wait(barrier, n_par + n_arc - 2)

    def share_of(device):
        return pl.ds(pl.multiple_of(device * share, 8), share)

    def part_copy(i):
        peer = par_peer(i)
        return send(part_ref.at[share_of(peer), :PANEL], piece_ref.at[i, :, :PANEL], part_sems, 0, {"par": peer})

    def both_copy(i):
        peer = par_peer(i)
        return send(part_ref.at[share_of(peer)], piece_ref.at[i], part_sems, 1, {"par": peer})

    def parts(count):
        some = piece_ref.at[:count, :, :PANEL]
        return send(some, some, part_sems, 0, {"par": par_peer(0)})

    def obs_copy():
        there = pl.ds(pl.multiple_of((1 - core) * (cols // 2), BLK), cols // 2)
        return send(obs_ref.at[:, there], other_obs_ref, core_sems, 0, sibling)

    def sibling_panel_copy():
        return send(panel_ref, other_panel_ref, core_sems, 1, sibling)

    owns_last = par == n_par - 1
    own_share = share_of(par)

    @pl.when(owns_last)
    def _():
        part_ref[:, PANEL:] = obs_ref[:, cols - PANEL:]
        each(n_par - 1, lambda i: both_copy(i).start())

    @pl.when(jnp.logical_not(owns_last))
    def _():
        each(n_par - 1, lambda i: part_copy(i).start())

    obs_copy().start()

    @pl.when(owns_last)
    def _():
        parts(n_par - 1).wait_recv()
        panel_ref[own_share, PANEL:] = part_ref[own_share, PANEL:]

    @pl.when(jnp.logical_not(owns_last))
    def _():
        parts(n_par - 2).wait_recv()
        both_copy(par).wait_recv()
        panel_ref[own_share, PANEL:] = piece_ref[par, :, PANEL:]

    total = part_ref[own_share, :PANEL]
    for i in range(n_par - 1):
        total = total + piece_ref[i, :, :PANEL]
    panel_ref[own_share, :PANEL] = total

    def panel_copy(i):
        return send(panel_ref.at[own_share], panel_ref.at[own_share], panel_sems, 0, {"par": par_peer(i)})

    def panel_all():
        others = panel_ref.at[:share * (n_par - 1)]
        return send(others, others, panel_sems, 0, {"par": par_peer(0)})

    each(n_par - 1, lambda i: panel_copy(i).start())
    panel_all().wait_recv()
    sibling_panel_copy().start()

    def in_order(ref):
        one, two = ref[:, :PANEL], ref[:, PANEL:]
        return jnp.concatenate([jnp.where(last_first, two, one), jnp.where(last_first, one, two)], 1)

    panel = in_order(panel_ref)
    turned = panel.T
    for i in range(tiles):
        gram_rows = dot_nn(turned[i * TILE:(i + 1) * TILE], panel[:, :(i + 1) * TILE])
        for j in range(i + 1):
            at = (i * (i + 1) // 2 + j) * TILE
            gram_ref[at:at + TILE, :] = gram_rows[:, j * TILE:(j + 1) * TILE]

    def gram_copy(i):
        peer = arc_peer(i)
        at = pl.multiple_of((2 * par + peer % 2) * slice_rows, 8)
        return send(gram_ref.at[pl.ds(at, slice_rows)], gram_piece_ref.at[i], gram_sems, i, {"arc": peer})

    each(n_arc - 1, lambda i: gram_copy(i).start())

    def fill_stack(at, turned_panel):
        high, low = halves(turned_panel)
        stack_ref[:, at:at + 3 * rows] = jnp.concatenate([high, high, low], 1)

    fill_stack(0, turned)
    sibling_panel_copy().wait_recv()
    fill_stack(3 * rows, in_order(other_panel_ref).T)

    def owner_chip(t):
        side = t % 2
        across = chips - 1 - chip
        beside = chip + 1 - 2 * (chip % 2)
        return [
            (lax.rem(chip + 2, chips), lax.rem(chip + 2, chips)),
            (beside, across),
            (across, beside),
            (chip, chip),
        ][t // 2][side]

    def column_of(t):
        return pl.multiple_of(((t % 2) * 4 + owner_chip(t)) * width, BLK)

    def cross_tile(t):
        own = obs_ref[:, pl.ds(pl.multiple_of(core * (cols // 2) + column_of(t), BLK), width)]
        theirs = other_obs_ref[:, pl.ds(column_of(t), width)]
        up, down = halves(own)
        their_up, their_down = halves(theirs)
        stacked = jnp.concatenate([up, down, up, their_up, their_down, their_up], 0)
        return jnp.dot(stack_ref[...], stacked, preferred_element_type=F32)

    def one_copy(t):
        to = (chip + 1 - 2 * (chip % 2)) if t % 2 == 0 else (chips - 1 - chip)
        return send(sums_ref.at[t], from_one_ref.at[t], one_sems, t, {"arc": 2 * to + core})

    obs_copy().wait_recv()
    for t in range(4):
        sums_ref[t] = cross_tile(t)
        one_copy(t).start()

    each(n_arc - 1, lambda i: gram_copy(i).wait_recv())
    own_at = pl.multiple_of((2 * par + core) * slice_rows, 8)
    gram_total = gram_ref[pl.ds(own_at, slice_rows), :]
    for i in range(n_arc - 1):
        gram_total = gram_total + gram_piece_ref[i]
    gram_all_ref[par, core] = gram_total

    def all_copy(i):
        here = gram_all_ref.at[par, core]
        return send(here, here, all_sems, 0, {"par": par_peer(i)})

    def all_all():
        others = gram_all_ref.at[:n_par - 1, core]
        return send(others, others, all_sems, 0, {"par": par_peer(0)})

    each(n_par - 1, lambda i: all_copy(i).start())

    for t in range(4, 8):
        sums_ref[t] = cross_tile(t)

    all_all().wait_recv()
    fwd = send(gram_all_ref.at[:, core], gram_all_ref.at[:, core], core_sems, 2, sibling)
    fwd.start()
    fwd.wait_recv()
    flat = gram_all_ref[...].reshape(2 * n_par * slice_rows, TILE)
    for i in range(tiles):
        for j in range(i + 1):
            at = (i * (i + 1) // 2 + j) * TILE
            fac_ref[i * TILE:(i + 1) * TILE, j * TILE:(j + 1) * TILE] = flat[at:at + TILE]
        if i + 1 < tiles:
            fac_ref[i * TILE:(i + 1) * TILE, (i + 1) * TILE:] = jnp.zeros((TILE, order - (i + 1) * TILE), F32)

    part = width // 2

    def two_copy(t, h):
        to = (chips - 1 - chip) if t % 2 == 0 else (chip + 1 - 2 * (chip % 2))
        columns = pl.ds(h * part, part)
        return send(
            sums_ref.at[4 + t, :, columns], from_two_ref.at[t, :, columns], two_sems, 2 * t + h, {"arc": 2 * to + core}
        )

    for k in range(tiles):
        factor_step(fac_ref, k, tiles)
        if k == 1:
            for t in range(2):
                one_copy(t).wait_recv()
                sums_ref[4 + t] = sums_ref[4 + t] + from_one_ref[t]
                two_copy(t, 0).start()
            for t in range(2):
                two_copy(t, 1).start()

    def out_column(t, h):
        return pl.multiple_of(core * (cols // 2) + column_of(6 + t) + h * part, BLK)

    def out_copy(t, h, i):
        peer = arc_peer(i)
        src = result_ref.at[t, pl.ds(pl.multiple_of(peer * out_rows, 8), out_rows), h * part:(h + 1) * part]
        dst = out_ref.at[:, pl.ds(out_column(t, h), part)]
        return send(src, dst, out_sems, (2 * t + h) * (n_arc - 1) + i, {"arc": peer})

    for h in range(2):
        for t in range(2):
            left, right = h * part, (h + 1) * part
            if h == 0:
                one_copy(2 + t).wait_recv()
            two_copy(t, h).wait_recv()
            whole = sums_ref[6 + t, :, left:right] + from_one_ref[2 + t, :, left:right] + from_two_ref[t, :, left:right]
            for i in range(tiles):
                depth = (i + 1) * TILE
                result_ref[t, i * TILE:depth, left:right] = dot_nn(fac_ref[i * TILE:depth, :depth], whole[:depth]) * scale
            each(n_arc - 1, lambda i: out_copy(t, h, i).start())
            out_ref[:, pl.ds(out_column(t, h), part)] = result_ref[
                t, pl.ds(pl.multiple_of(arc * out_rows, 8), out_rows), left:right
            ]

    @pl.when(owns_last)
    def _():
        send(piece_ref, piece_ref, part_sems, 1, {"par": par_peer(0)}).wait_send()

    @pl.when(jnp.logical_not(owns_last))
    def _():
        parts(n_par - 1).wait_send()

    panel_all().wait_send()
    each(n_arc - 1, lambda i: gram_copy(i).wait_send())
    all_all().wait_send()
    fwd.wait_send()
    obs_copy().wait_send()
    sibling_panel_copy().wait_send()

    for t in range(4):
        one_copy(t).wait_send()
    for t in range(2):
        for h in range(2):
            two_copy(t, h).wait_send()
            each(n_arc - 1, lambda i: out_copy(t, h, i).wait())


def shards(observations, arc_mask, panel_owner):
    n_arc, n_par = lax.axis_size("arc"), lax.axis_size("par")
    rows, cols = observations.shape
    order = 2 * PANEL
    share = rows // n_par
    width = cols // 16
    tiles = order // TILE
    slice_rows = tiles * (tiles + 1) // 2 * TILE // (2 * n_par)

    def pair(count):
        return pltpu.SemaphoreType.DMA((2, count))

    return pl.pallas_call(
        functools.partial(kernel, n_arc, n_par),
        out_shape=jax.ShapeDtypeStruct((order // n_arc, cols), F32),
        in_specs=[pl.BlockSpec(memory_space=pl.ANY)] * 3,
        out_specs=pl.BlockSpec(memory_space=pltpu.VMEM),
        scratch_shapes=[
            pltpu.VMEM((rows, cols), F32),
            pltpu.SMEM(arc_mask.shape, jnp.int32),
            pltpu.SMEM(panel_owner.shape, jnp.int32),
            pltpu.VMEM((rows, order), F32),
            pltpu.VMEM((n_par - 1, share, order), F32),
            pltpu.VMEM((rows, order), F32),
            pltpu.VMEM((rows, cols // 2), F32),
            pltpu.VMEM((rows, order), F32),
            pltpu.VMEM((order, 6 * rows), BF16),
            pltpu.VMEM((2 * n_par * slice_rows, TILE), F32),
            pltpu.VMEM((n_arc - 1, slice_rows, TILE), F32),
            pltpu.VMEM((n_par, 2, slice_rows, TILE), F32),
            pltpu.VMEM((order, order), F32),
            pltpu.VMEM((8, order, width), F32),
            pltpu.VMEM((4, order, width), F32),
            pltpu.VMEM((2, order, width), F32),
            pltpu.VMEM((2, order, width), F32),
            pltpu.SemaphoreType.DMA((3,)),
            pair(2),
            pair(1),
            pair(n_arc - 1),
            pair(1),
            pair(3),
            pair(4),
            pair(4),
            pair(4 * (n_arc - 1)),
        ],
        compiler_params=pltpu.CompilerParams(
            collective_id=0, has_side_effects=True, vmem_limit_bytes=60 << 20
        ),
        name="info_rows",
    )(observations, arc_mask, panel_owner)


def solution(mesh):
    return jax.shard_map(
        shards,
        mesh=mesh,
        in_specs=(P("arc", "par"), P("arc", "par"), P()),
        out_specs=P("arc", "par"),
        check_vma=False,
    )
```

```python
import functools
import math

import jax
import jax.numpy as jnp
from jax import lax
from jax.experimental import pallas as pl
from jax.experimental.pallas import tpu as pltpu
from jax.sharding import PartitionSpec as P

PANEL = 256
BLK = 128
TILE = 128
HIGHEST = lax.Precision.HIGHEST
MESH = pl.DeviceIdType.MESH
F32 = jnp.float32
BF16 = jnp.bfloat16


def dot_nt(left, right):
    return lax.dot_general(left, right, (((1,), (1,)), ((), ())), precision=HIGHEST, preferred_element_type=F32)


def dot_nn(left, right):
    return jnp.dot(left, right, precision=HIGHEST, preferred_element_type=F32)


def halves(value):
    high = value.astype(BF16)
    return high, (value - high.astype(F32)).astype(BF16)


def tile_inverse(tile, width=8):
    lanes = lax.broadcasted_iota(jnp.int32, (8, TILE), 1)
    subl = lax.broadcasted_iota(jnp.int32, (8, TILE), 0)
    zero = jnp.zeros((8, TILE), F32)
    done = []
    tail = tile
    for start in range(0, TILE, width):
        base = start // 8
        size = TILE - 8 * base - 8
        head, tail = tail[:8], tail[8:]
        tail_lanes = lax.broadcasted_iota(jnp.int32, (size, TILE), 1) if size else None
        head_cols = [jnp.broadcast_to(head[:, start + c:start + c + 1], (8, TILE)) for c in range(width)]
        tail_cols = [jnp.broadcast_to(tail[:, start + c:start + c + 1], (size, TILE)) for c in range(width)] if size else None
        for c in range(width):
            col = start + c
            pivot = jnp.broadcast_to(head_cols[c][c:c + 1, :], (8, TILE))
            inv = 1.0 / pivot
            on_col = lanes == col
            prow = jnp.where(on_col, inv, jnp.broadcast_to(head[c:c + 1, :], (8, TILE)) * inv)
            below = subl > c
            mult = jnp.where(below, head_cols[c], zero)
            coefs = [jnp.broadcast_to(head_cols[d][c:c + 1, :], (8, TILE)) * inv for d in range(c + 1, width)]
            for d in range(c + 1, width):
                head_cols[d] = head_cols[d] - mult * coefs[d - c - 1]
            head = jnp.where(on_col, jnp.where(below, zero, jnp.where(subl == c, pivot, head)), head) - mult * prow
            if size:
                for d in range(c + 1, width):
                    tail_cols[d] = tail_cols[d] - tail_cols[c] * jnp.broadcast_to(coefs[d - c - 1][:1], (size, TILE))
                tail = jnp.where(tail_lanes == col, 0.0, tail) - tail_cols[c] * jnp.broadcast_to(prow[:1], (size, TILE))
        on_diag = lanes == subl + start
        diag = jnp.sum(jnp.where(on_diag, head, zero), axis=1, keepdims=True)
        scaled = jnp.where(on_diag, 1.0, head) * lax.rsqrt(diag)
        done.append(jnp.where(lanes <= subl + start, scaled, zero))
    return jnp.concatenate(done, 0)


def factor_step(ref, k, count):
    low, top = k * TILE, (k + 1) * TILE
    inv = tile_inverse(ref[low:top, low:top])
    ref[low:top, low:top] = inv
    if k:
        ref[low:top, :low] = dot_nn(inv, ref[low:top, :low])
    if k + 1 < count:
        below = dot_nt(ref[top:, low:top], inv)
        for i in range(k + 1, count):
            part = below[(i - k - 1) * TILE:(i - k) * TILE]
            ref[i * TILE:(i + 1) * TILE, top:(i + 1) * TILE] -= dot_nt(part, below[:(i - k) * TILE])
        if k:
            ref[top:, :low] -= dot_nn(below, ref[low:top, :low])
        ref[top:, low:top] = -dot_nn(below, inv)


def kernel(
    n_arc, n_par,
    obs_hbm, mask_hbm, owner_hbm, out_ref,
    obs_ref, mask_ref, owner_ref,
    part_ref, piece_ref, panel_ref, other_obs_ref, other_panel_ref, turned_ref, stack_ref,
    gram_ref, gram_piece_ref, gram_all_ref, fac_ref,
    sums_ref, from_one_ref, from_two_ref, result_ref,
    load_sems, part_sems, panel_sems, gram_sems, all_sems, core_sems, one_sems, two_sems, out_sems,
):
    rows, cols = obs_ref.shape
    order = 2 * PANEL
    share = rows // n_par
    slice_rows = gram_piece_ref.shape[1]
    width = cols // 16
    out_rows = out_ref.shape[0]
    tiles = order // TILE
    chips = n_arc // 2
    scale = 1.0 / math.sqrt(rows * n_arc)
    arc = lax.axis_index("arc")
    par = lax.axis_index("par")
    chip = arc // 2
    core = arc % 2

    def send(src, dst, sems, slot, target):
        return pltpu.make_async_remote_copy(
            src_ref=src, dst_ref=dst, send_sem=sems.at[0, slot], recv_sem=sems.at[1, slot],
            device_id=target, device_id_type=MESH,
        )

    def each(count, body):
        lax.fori_loop(0, count, lambda i, carry: (body(i), carry)[1], 0)

    def par_peer(i):
        return lax.rem(par + lax.rem(i * 4, n_par - 1) + 1, n_par)

    def arc_peer(i):
        return lax.rem(arc + i + 1, n_arc)

    sibling = {"arc": arc + 1 - 2 * core}
    loads = [
        pltpu.make_async_copy(src, dst, load_sems.at[i])
        for i, (src, dst) in enumerate([(mask_hbm, mask_ref), (owner_hbm, owner_ref), (obs_hbm, obs_ref)])
    ]
    for load in loads:
        load.start()

    barrier = pltpu.get_barrier_semaphore()
    each(n_par - 1, lambda i: pl.semaphore_signal(barrier, inc=1, device_id={"par": par_peer(i)}, device_id_type=MESH))
    each(n_arc - 1, lambda i: pl.semaphore_signal(barrier, inc=1, device_id={"arc": arc_peer(i)}, device_id_type=MESH))
    for load in loads:
        load.wait()

    held = cols // PANEL
    last = n_par * held - 1
    last_first = owner_ref[0] == last
    other = jnp.where(last_first, owner_ref[1], owner_ref[0])
    chosen = [jnp.where(other == par * held + b, 1.0, 0.0) for b in range(held)]
    for half in range(PANEL // BLK):
        for band in range(rows // BLK):
            low, top = band * BLK, (band + 1) * BLK
            total = jnp.zeros((BLK, BLK), F32)
            for b in range(held):
                block = b * (PANEL // BLK) + half
                left, right = block * BLK, (block + 1) * BLK
                masked = obs_ref[low:top, left:right] * mask_ref[band, block].astype(F32)
                obs_ref[low:top, left:right] = masked
                total = total + masked * chosen[b]
            part_ref[low:top, half * BLK:(half + 1) * BLK] = total

    pl.semaphore_wait(barrier, n_par + n_arc - 2)

    def share_of(device):
        return pl.ds(pl.multiple_of(device * share, 8), share)

    def part_copy(i):
        peer = par_peer(i)
        return send(part_ref.at[share_of(peer), :PANEL], piece_ref.at[i, :, :PANEL], part_sems, 0, {"par": peer})

    def both_copy(i):
        peer = par_peer(i)
        return send(part_ref.at[share_of(peer)], piece_ref.at[i], part_sems, 1, {"par": peer})

    def parts(count):
        some = piece_ref.at[:count, :, :PANEL]
        return send(some, some, part_sems, 0, {"par": par_peer(0)})

    def obs_copy():
        there = pl.ds(pl.multiple_of((1 - core) * (cols // 2), BLK), cols // 2)
        return send(obs_ref.at[:, there], other_obs_ref, core_sems, 0, sibling)

    def sibling_panel_copy():
        return send(panel_ref, other_panel_ref, core_sems, 1, sibling)

    owns_last = par == n_par - 1
    own_share = share_of(par)

    @pl.when(owns_last)
    def _():
        part_ref[:, PANEL:] = obs_ref[:, cols - PANEL:]
        each(n_par - 1, lambda i: both_copy(i).start())

    @pl.when(jnp.logical_not(owns_last))
    def _():
        each(n_par - 1, lambda i: part_copy(i).start())

    obs_copy().start()

    @pl.when(owns_last)
    def _():
        parts(n_par - 1).wait_recv()
        panel_ref[own_share, PANEL:] = part_ref[own_share, PANEL:]

    @pl.when(jnp.logical_not(owns_last))
    def _():
        parts(n_par - 2).wait_recv()
        slot = lax.rem(par * 4, n_par - 1)
        both_copy(slot).wait_recv()
        panel_ref[own_share, PANEL:] = piece_ref[slot, :, PANEL:]

    total = part_ref[own_share, :PANEL]
    for i in range(n_par - 1):
        total = total + piece_ref[i, :, :PANEL]
    panel_ref[own_share, :PANEL] = total

    def panel_copy(i):
        return send(panel_ref.at[own_share], panel_ref.at[own_share], panel_sems, 0, {"par": par_peer(i)})

    def panel_all():
        others = panel_ref.at[:share * (n_par - 1)]
        return send(others, others, panel_sems, 0, {"par": par_peer(0)})

    each(n_par - 1, lambda i: panel_copy(i).start())
    panel_all().wait_recv()
    sibling_panel_copy().start()

    def in_order(ref):
        one, two = ref[:, :PANEL], ref[:, PANEL:]
        return jnp.concatenate([jnp.where(last_first, two, one), jnp.where(last_first, one, two)], 1)

    panel = in_order(panel_ref)
    turned = panel.T
    turned_ref[...] = turned
    band_rows = TILE // n_par
    picked = [turned_ref[pl.ds(pl.multiple_of(i * TILE + par * band_rows, 8), band_rows), :] for i in range(tiles)]
    gram_rows = dot_nn(jnp.concatenate(picked, 0), panel)
    for i in range(tiles):
        for j in range(i + 1):
            at = (i * (i + 1) // 2 + j) * band_rows
            gram_ref[at:at + band_rows, :] = gram_rows[i * band_rows:(i + 1) * band_rows, j * TILE:(j + 1) * TILE]

    def gram_copy(i):
        peer = arc_peer(i)
        at = pl.multiple_of(peer % 2 * slice_rows, 8)
        return send(gram_ref.at[pl.ds(at, slice_rows)], gram_piece_ref.at[i], gram_sems, i, {"arc": peer})

    each(n_arc - 1, lambda i: gram_copy(i).start())

    def fill_stack(at, turned_panel):
        high, low = halves(turned_panel)
        stack_ref[:, at:at + 3 * rows] = jnp.concatenate([high, high, low], 1)

    fill_stack(0, turned)
    sibling_panel_copy().wait_recv()
    fill_stack(3 * rows, in_order(other_panel_ref).T)

    def owner_chip(t):
        side = t % 2
        across = chips - 1 - chip
        beside = chip + 1 - 2 * (chip % 2)
        return [
            (lax.rem(chip + 2, chips), lax.rem(chip + 2, chips)),
            (beside, across),
            (across, beside),
            (chip, chip),
        ][t // 2][side]

    def column_of(t):
        return pl.multiple_of(((t % 2) * 4 + owner_chip(t)) * width, BLK)

    def cross_tile(t):
        own = obs_ref[:, pl.ds(pl.multiple_of(core * (cols // 2) + column_of(t), BLK), width)]
        theirs = other_obs_ref[:, pl.ds(column_of(t), width)]
        up, down = halves(own)
        their_up, their_down = halves(theirs)
        stacked = jnp.concatenate([up, down, up, their_up, their_down, their_up], 0)
        return jnp.dot(stack_ref[...], stacked, preferred_element_type=F32)

    def one_copy(t):
        to = (chip + 1 - 2 * (chip % 2)) if t % 2 == 0 else (chips - 1 - chip)
        return send(sums_ref.at[t], from_one_ref.at[t], one_sems, t, {"arc": 2 * to + core})

    obs_copy().wait_recv()
    for t in range(4):
        sums_ref[t] = cross_tile(t)
        one_copy(t).start()

    each(n_arc - 1, lambda i: gram_copy(i).wait_recv())
    own_at = pl.multiple_of(core * slice_rows, 8)
    gram_total = gram_ref[pl.ds(own_at, slice_rows), :]
    for i in range(n_arc - 1):
        gram_total = gram_total + gram_piece_ref[i]
    gram_all_ref[par, core] = gram_total

    def all_copy(i):
        here = gram_all_ref.at[par, core]
        return send(here, here, all_sems, 0, {"par": par_peer(i)})

    def all_all():
        others = gram_all_ref.at[:n_par - 1, core]
        return send(others, others, all_sems, 0, {"par": par_peer(0)})

    each(n_par - 1, lambda i: all_copy(i).start())

    for t in range(4, 8):
        sums_ref[t] = cross_tile(t)

    all_all().wait_recv()
    fwd = send(gram_all_ref.at[:, core], gram_all_ref.at[:, core], core_sems, 2, sibling)
    fwd.start()
    fwd.wait_recv()
    for i in range(tiles):
        for j in range(i + 1):
            half, at = divmod((i * (i + 1) // 2 + j) * band_rows, slice_rows)
            block = gram_all_ref[:, half, at:at + band_rows, :].reshape(TILE, TILE)
            fac_ref[i * TILE:(i + 1) * TILE, j * TILE:(j + 1) * TILE] = block
        if i + 1 < tiles:
            fac_ref[i * TILE:(i + 1) * TILE, (i + 1) * TILE:] = jnp.zeros((TILE, order - (i + 1) * TILE), F32)

    part = width // 2

    def two_copy(t, h):
        to = (chips - 1 - chip) if t % 2 == 0 else (chip + 1 - 2 * (chip % 2))
        columns = pl.ds(h * part, part)
        return send(
            sums_ref.at[4 + t, :, columns], from_two_ref.at[t, :, columns], two_sems, 2 * t + h, {"arc": 2 * to + core}
        )

    for k in range(tiles):
        factor_step(fac_ref, k, tiles)
        if k == 1:
            for t in range(2):
                one_copy(t).wait_recv()
                sums_ref[4 + t] = sums_ref[4 + t] + from_one_ref[t]
                two_copy(t, 0).start()
            for t in range(2):
                two_copy(t, 1).start()

    def out_column(t, h):
        return pl.multiple_of(core * (cols // 2) + column_of(6 + t) + h * part, BLK)

    def out_copy(t, h, i):
        peer = arc_peer(i)
        src = result_ref.at[t, pl.ds(pl.multiple_of(peer * out_rows, 8), out_rows), h * part:(h + 1) * part]
        dst = out_ref.at[:, pl.ds(out_column(t, h), part)]
        return send(src, dst, out_sems, (2 * t + h) * (n_arc - 1) + i, {"arc": peer})

    for h in range(2):
        for t in range(2):
            left, right = h * part, (h + 1) * part
            if h == 0:
                one_copy(2 + t).wait_recv()
            two_copy(t, h).wait_recv()
            whole = sums_ref[6 + t, :, left:right] + from_one_ref[2 + t, :, left:right] + from_two_ref[t, :, left:right]
            for i in range(tiles):
                depth = (i + 1) * TILE
                result_ref[t, i * TILE:depth, left:right] = dot_nn(fac_ref[i * TILE:depth, :depth], whole[:depth]) * scale
            each(n_arc - 1, lambda i: out_copy(t, h, i).start())
            out_ref[:, pl.ds(out_column(t, h), part)] = result_ref[
                t, pl.ds(pl.multiple_of(arc * out_rows, 8), out_rows), left:right
            ]

    @pl.when(owns_last)
    def _():
        send(piece_ref, piece_ref, part_sems, 1, {"par": par_peer(0)}).wait_send()

    @pl.when(jnp.logical_not(owns_last))
    def _():
        parts(n_par - 1).wait_send()

    panel_all().wait_send()
    each(n_arc - 1, lambda i: gram_copy(i).wait_send())
    all_all().wait_send()
    fwd.wait_send()
    obs_copy().wait_send()
    sibling_panel_copy().wait_send()

    for t in range(4):
        one_copy(t).wait_send()
    for t in range(2):
        for h in range(2):
            two_copy(t, h).wait_send()
            each(n_arc - 1, lambda i: out_copy(t, h, i).wait())


def shards(observations, arc_mask, panel_owner):
    n_arc, n_par = lax.axis_size("arc"), lax.axis_size("par")
    rows, cols = observations.shape
    order = 2 * PANEL
    share = rows // n_par
    width = cols // 16
    tiles = order // TILE
    slice_rows = tiles * (tiles + 1) // 2 * TILE // (2 * n_par)

    def pair(count):
        return pltpu.SemaphoreType.DMA((2, count))

    return pl.pallas_call(
        functools.partial(kernel, n_arc, n_par),
        out_shape=jax.ShapeDtypeStruct((order // n_arc, cols), F32),
        in_specs=[pl.BlockSpec(memory_space=pl.ANY)] * 3,
        out_specs=pl.BlockSpec(memory_space=pltpu.VMEM),
        scratch_shapes=[
            pltpu.VMEM((rows, cols), F32),
            pltpu.SMEM(arc_mask.shape, jnp.int32),
            pltpu.SMEM(panel_owner.shape, jnp.int32),
            pltpu.VMEM((rows, order), F32),
            pltpu.VMEM((n_par - 1, share, order), F32),
            pltpu.VMEM((rows, order), F32),
            pltpu.VMEM((rows, cols // 2), F32),
            pltpu.VMEM((rows, order), F32),
            pltpu.VMEM((order, rows), F32),
            pltpu.VMEM((order, 6 * rows), BF16),
            pltpu.VMEM((2 * slice_rows, TILE), F32),
            pltpu.VMEM((n_arc - 1, slice_rows, TILE), F32),
            pltpu.VMEM((n_par, 2, slice_rows, TILE), F32),
            pltpu.VMEM((order, order), F32),
            pltpu.VMEM((8, order, width), F32),
            pltpu.VMEM((4, order, width), F32),
            pltpu.VMEM((2, order, width), F32),
            pltpu.VMEM((2, order, width), F32),
            pltpu.SemaphoreType.DMA((3,)),
            pair(2),
            pair(1),
            pair(n_arc - 1),
            pair(1),
            pair(3),
            pair(4),
            pair(4),
            pair(4 * (n_arc - 1)),
        ],
        compiler_params=pltpu.CompilerParams(
            collective_id=0, has_side_effects=True, vmem_limit_bytes=60 << 20
        ),
        name="info_rows",
    )(observations, arc_mask, panel_owner)


def solution(mesh):
    return jax.shard_map(
        shards,
        mesh=mesh,
        in_specs=(P("arc", "par"), P("arc", "par"), P()),
        out_specs=P("arc", "par"),
        check_vma=False,
    )
```

```python
import functools
import math

import jax
import jax.numpy as jnp
from jax import lax
from jax.experimental import pallas as pl
from jax.experimental.pallas import tpu as pltpu
from jax.sharding import PartitionSpec as P

PANEL = 256
BLK = 128
TILE = 128
HIGHEST = lax.Precision.HIGHEST
MESH = pl.DeviceIdType.MESH
F32 = jnp.float32
BF16 = jnp.bfloat16


def dot_nt(left, right):
    return lax.dot_general(left, right, (((1,), (1,)), ((), ())), precision=HIGHEST, preferred_element_type=F32)


def dot_nn(left, right):
    return jnp.dot(left, right, precision=HIGHEST, preferred_element_type=F32)


def halves(value):
    high = value.astype(BF16)
    return high, (value - high.astype(F32)).astype(BF16)


def tile_inverse(tile, width=8):
    lanes = lax.broadcasted_iota(jnp.int32, (8, TILE), 1)
    subl = lax.broadcasted_iota(jnp.int32, (8, TILE), 0)
    zero = jnp.zeros((8, TILE), F32)
    done = []
    tail = tile
    for start in range(0, TILE, width):
        base = start // 8
        size = TILE - 8 * base - 8
        head, tail = tail[:8], tail[8:]
        tail_lanes = lax.broadcasted_iota(jnp.int32, (size, TILE), 1) if size else None
        head_cols = [jnp.broadcast_to(head[:, start + c:start + c + 1], (8, TILE)) for c in range(width)]
        tail_cols = [jnp.broadcast_to(tail[:, start + c:start + c + 1], (size, TILE)) for c in range(width)] if size else None
        for c in range(width):
            col = start + c
            pivot = jnp.broadcast_to(head_cols[c][c:c + 1, :], (8, TILE))
            inv = 1.0 / pivot
            on_col = lanes == col
            prow = jnp.where(on_col, inv, jnp.broadcast_to(head[c:c + 1, :], (8, TILE)) * inv)
            below = subl > c
            mult = jnp.where(below, head_cols[c], zero)
            coefs = [jnp.broadcast_to(head_cols[d][c:c + 1, :], (8, TILE)) * inv for d in range(c + 1, width)]
            for d in range(c + 1, width):
                head_cols[d] = head_cols[d] - mult * coefs[d - c - 1]
            head = jnp.where(on_col, jnp.where(below, zero, jnp.where(subl == c, pivot, head)), head) - mult * prow
            if size:
                for d in range(c + 1, width):
                    tail_cols[d] = tail_cols[d] - tail_cols[c] * jnp.broadcast_to(coefs[d - c - 1][:1], (size, TILE))
                tail = jnp.where(tail_lanes == col, 0.0, tail) - tail_cols[c] * jnp.broadcast_to(prow[:1], (size, TILE))
        on_diag = lanes == subl + start
        diag = jnp.sum(jnp.where(on_diag, head, zero), axis=1, keepdims=True)
        scaled = jnp.where(on_diag, 1.0, head) * lax.rsqrt(diag)
        done.append(jnp.where(lanes <= subl + start, scaled, zero))
    return jnp.concatenate(done, 0)


def factor_step(ref, k, count):
    low, top = k * TILE, (k + 1) * TILE
    inv = tile_inverse(ref[low:top, low:top])
    ref[low:top, low:top] = inv
    if k:
        ref[low:top, :low] = dot_nn(inv, ref[low:top, :low])
    if k + 1 < count:
        below = dot_nt(ref[top:, low:top], inv)
        for i in range(k + 1, count):
            part = below[(i - k - 1) * TILE:(i - k) * TILE]
            ref[i * TILE:(i + 1) * TILE, top:(i + 1) * TILE] -= dot_nt(part, below[:(i - k) * TILE])
        if k:
            ref[top:, :low] -= dot_nn(below, ref[low:top, :low])
        ref[top:, low:top] = -dot_nn(below, inv)


def kernel(
    n_arc, n_par,
    obs_hbm, mask_hbm, owner_hbm, out_ref,
    obs_ref, mask_ref, owner_ref,
    part_ref, piece_ref, panel_ref, other_obs_ref, other_panel_ref, turned_ref, stack_ref,
    gram_ref, gram_piece_ref, gram_all_ref, fac_ref,
    sums_ref, from_one_ref, from_two_ref, result_ref,
    load_sems, part_sems, panel_sems, gram_sems, all_sems, core_sems, one_sems, two_sems, out_sems,
):
    rows, cols = obs_ref.shape
    order = 2 * PANEL
    share = rows // n_par
    slice_rows = gram_piece_ref.shape[1]
    width = cols // 16
    out_rows = out_ref.shape[0]
    tiles = order // TILE
    chips = n_arc // 2
    scale = 1.0 / math.sqrt(rows * n_arc)
    arc = lax.axis_index("arc")
    par = lax.axis_index("par")
    chip = arc // 2
    core = arc % 2

    def send(src, dst, sems, slot, target):
        return pltpu.make_async_remote_copy(
            src_ref=src, dst_ref=dst, send_sem=sems.at[0, slot], recv_sem=sems.at[1, slot],
            device_id=target, device_id_type=MESH,
        )

    def each(count, body):
        lax.fori_loop(0, count, lambda i, carry: (body(i), carry)[1], 0)

    def par_peer(i):
        return lax.rem(par + lax.rem(i * 4, n_par - 1) + 1, n_par)

    def arc_peer(i):
        return lax.rem(arc + i + 1, n_arc)

    sibling = {"arc": arc + 1 - 2 * core}
    loads = [
        pltpu.make_async_copy(src, dst, load_sems.at[i])
        for i, (src, dst) in enumerate([(mask_hbm, mask_ref), (owner_hbm, owner_ref), (obs_hbm, obs_ref)])
    ]
    for load in loads:
        load.start()

    barrier = pltpu.get_barrier_semaphore()
    each(n_par - 1, lambda i: pl.semaphore_signal(barrier, inc=1, device_id={"par": par_peer(i)}, device_id_type=MESH))
    each(n_arc - 1, lambda i: pl.semaphore_signal(barrier, inc=1, device_id={"arc": arc_peer(i)}, device_id_type=MESH))
    for load in loads:
        load.wait()

    held = cols // PANEL
    last = n_par * held - 1
    last_first = owner_ref[0] == last
    other = jnp.where(last_first, owner_ref[1], owner_ref[0])
    chosen = [jnp.where(other == par * held + b, 1.0, 0.0) for b in range(held)]
    for half in range(PANEL // BLK):
        for band in range(rows // BLK):
            low, top = band * BLK, (band + 1) * BLK
            total = jnp.zeros((BLK, BLK), F32)
            for b in range(held):
                block = b * (PANEL // BLK) + half
                left, right = block * BLK, (block + 1) * BLK
                masked = obs_ref[low:top, left:right] * mask_ref[band, block].astype(F32)
                obs_ref[low:top, left:right] = masked
                total = total + masked * chosen[b]
            part_ref[low:top, half * BLK:(half + 1) * BLK] = total

    pl.semaphore_wait(barrier, n_par + n_arc - 2)

    def share_of(device):
        return pl.ds(pl.multiple_of(device * share, 8), share)

    def part_copy(i):
        peer = par_peer(i)
        return send(part_ref.at[share_of(peer), :PANEL], piece_ref.at[i, :, :PANEL], part_sems, 0, {"par": peer})

    def both_copy(i):
        peer = par_peer(i)
        return send(part_ref.at[share_of(peer)], piece_ref.at[i], part_sems, 1, {"par": peer})

    def parts(count):
        some = piece_ref.at[:count, :, :PANEL]
        return send(some, some, part_sems, 0, {"par": par_peer(0)})

    def obs_copy():
        there = pl.ds(pl.multiple_of((1 - core) * (cols // 2), BLK), cols // 2)
        return send(obs_ref.at[:, there], other_obs_ref, core_sems, 0, sibling)

    def sibling_panel_copy():
        return send(panel_ref, other_panel_ref, core_sems, 1, sibling)

    owns_last = par == n_par - 1
    own_share = share_of(par)

    @pl.when(owns_last)
    def _():
        part_ref[:, PANEL:] = obs_ref[:, cols - PANEL:]
        each(n_par - 1, lambda i: both_copy(i).start())

    @pl.when(jnp.logical_not(owns_last))
    def _():
        each(n_par - 1, lambda i: part_copy(i).start())

    obs_copy().start()

    @pl.when(owns_last)
    def _():
        parts(n_par - 1).wait_recv()
        panel_ref[own_share, PANEL:] = part_ref[own_share, PANEL:]

    @pl.when(jnp.logical_not(owns_last))
    def _():
        parts(n_par - 2).wait_recv()
        slot = lax.rem(par * 4, n_par - 1)
        both_copy(slot).wait_recv()
        panel_ref[own_share, PANEL:] = piece_ref[slot, :, PANEL:]

    total = part_ref[own_share, :PANEL]
    for i in range(n_par - 1):
        total = total + piece_ref[i, :, :PANEL]
    panel_ref[own_share, :PANEL] = total

    def panel_copy(i):
        return send(panel_ref.at[own_share], panel_ref.at[own_share], panel_sems, 0, {"par": par_peer(i)})

    def panel_all():
        others = panel_ref.at[:share * (n_par - 1)]
        return send(others, others, panel_sems, 0, {"par": par_peer(0)})

    each(n_par - 1, lambda i: panel_copy(i).start())
    panel_all().wait_recv()
    sibling_panel_copy().start()

    def in_order(ref):
        one, two = ref[:, :PANEL], ref[:, PANEL:]
        return jnp.concatenate([jnp.where(last_first, two, one), jnp.where(last_first, one, two)], 1)

    panel = in_order(panel_ref)
    turned = panel.T
    turned_ref[...] = turned
    band_rows = TILE // n_par
    picked = [turned_ref[pl.ds(pl.multiple_of(i * TILE + par * band_rows, 8), band_rows), :] for i in range(tiles)]
    gram_rows = dot_nn(jnp.concatenate(picked, 0), panel)
    for i in range(tiles):
        for j in range(i + 1):
            at = (i * (i + 1) // 2 + j) * band_rows
            gram_ref[at:at + band_rows, :] = gram_rows[i * band_rows:(i + 1) * band_rows, j * TILE:(j + 1) * TILE]

    def gram_copy(i):
        peer = arc_peer(i)
        at = pl.multiple_of(peer % 2 * slice_rows, 8)
        return send(gram_ref.at[pl.ds(at, slice_rows)], gram_piece_ref.at[i], gram_sems, i, {"arc": peer})

    each(n_arc - 1, lambda i: gram_copy(i).start())

    def fill_stack(at, turned_panel):
        high, low = halves(turned_panel)
        stack_ref[:, at:at + 3 * rows] = jnp.concatenate([high, high, low], 1)

    fill_stack(0, turned)

    def owner_chip(t):
        side = t % 2
        across = chips - 1 - chip
        beside = chip + 1 - 2 * (chip % 2)
        return [
            (lax.rem(chip + 2, chips), lax.rem(chip + 2, chips)),
            (beside, across),
            (across, beside),
            (chip, chip),
        ][t // 2][side]

    def column_of(t):
        return pl.multiple_of(((t % 2) * 4 + owner_chip(t)) * width, BLK)

    def product(at, columns):
        up, down = halves(columns)
        return jnp.dot(stack_ref[:, at:at + 3 * rows], jnp.concatenate([up, down, up], 0), preferred_element_type=F32)

    def own_product(t):
        return product(0, obs_ref[:, pl.ds(pl.multiple_of(core * (cols // 2) + column_of(t), BLK), width)])

    def other_product(t):
        return product(3 * rows, other_obs_ref[:, pl.ds(column_of(t), width)])

    def one_copy(t):
        to = (chip + 1 - 2 * (chip % 2)) if t % 2 == 0 else (chips - 1 - chip)
        return send(sums_ref.at[t], from_one_ref.at[t], one_sems, t, {"arc": 2 * to + core})

    for t in range(4):
        sums_ref[t] = own_product(t)
    obs_copy().wait_recv()
    sibling_panel_copy().wait_recv()
    fill_stack(3 * rows, in_order(other_panel_ref).T)
    for t in range(4):
        sums_ref[t] = sums_ref[t] + other_product(t)
        one_copy(t).start()

    each(n_arc - 1, lambda i: gram_copy(i).wait_recv())
    own_at = pl.multiple_of(core * slice_rows, 8)
    gram_total = gram_ref[pl.ds(own_at, slice_rows), :]
    for i in range(n_arc - 1):
        gram_total = gram_total + gram_piece_ref[i]
    gram_all_ref[par, core] = gram_total

    def all_copy(i):
        here = gram_all_ref.at[par, core]
        return send(here, here, all_sems, 0, {"par": par_peer(i)})

    def all_all():
        others = gram_all_ref.at[:n_par - 1, core]
        return send(others, others, all_sems, 0, {"par": par_peer(0)})

    each(n_par - 1, lambda i: all_copy(i).start())

    for t in range(4, 8):
        sums_ref[t] = own_product(t) + other_product(t)

    all_all().wait_recv()
    fwd = send(gram_all_ref.at[:, core], gram_all_ref.at[:, core], core_sems, 2, sibling)
    fwd.start()
    fwd.wait_recv()
    for i in range(tiles):
        for j in range(i + 1):
            half, at = divmod((i * (i + 1) // 2 + j) * band_rows, slice_rows)
            block = gram_all_ref[:, half, at:at + band_rows, :].reshape(TILE, TILE)
            fac_ref[i * TILE:(i + 1) * TILE, j * TILE:(j + 1) * TILE] = block
        if i + 1 < tiles:
            fac_ref[i * TILE:(i + 1) * TILE, (i + 1) * TILE:] = jnp.zeros((TILE, order - (i + 1) * TILE), F32)

    part = width // 2

    def two_copy(t, h):
        to = (chips - 1 - chip) if t % 2 == 0 else (chip + 1 - 2 * (chip % 2))
        columns = pl.ds(h * part, part)
        return send(
            sums_ref.at[4 + t, :, columns], from_two_ref.at[t, :, columns], two_sems, 2 * t + h, {"arc": 2 * to + core}
        )

    for k in range(tiles):
        factor_step(fac_ref, k, tiles)
        if k == 1:
            for t in range(2):
                one_copy(t).wait_recv()
                sums_ref[4 + t] = sums_ref[4 + t] + from_one_ref[t]
                two_copy(t, 0).start()
            for t in range(2):
                two_copy(t, 1).start()

    def out_column(t, h):
        return pl.multiple_of(core * (cols // 2) + column_of(6 + t) + h * part, BLK)

    def out_copy(t, h, i):
        peer = arc_peer(i)
        src = result_ref.at[t, pl.ds(pl.multiple_of(peer * out_rows, 8), out_rows), h * part:(h + 1) * part]
        dst = out_ref.at[:, pl.ds(out_column(t, h), part)]
        return send(src, dst, out_sems, (2 * t + h) * (n_arc - 1) + i, {"arc": peer})

    for h in range(2):
        for t in range(2):
            left, right = h * part, (h + 1) * part
            if h == 0:
                one_copy(2 + t).wait_recv()
            two_copy(t, h).wait_recv()
            whole = sums_ref[6 + t, :, left:right] + from_one_ref[2 + t, :, left:right] + from_two_ref[t, :, left:right]
            for i in range(tiles):
                depth = (i + 1) * TILE
                result_ref[t, i * TILE:depth, left:right] = dot_nn(fac_ref[i * TILE:depth, :depth], whole[:depth]) * scale
            each(n_arc - 1, lambda i: out_copy(t, h, i).start())
            out_ref[:, pl.ds(out_column(t, h), part)] = result_ref[
                t, pl.ds(pl.multiple_of(arc * out_rows, 8), out_rows), left:right
            ]

    @pl.when(owns_last)
    def _():
        send(piece_ref, piece_ref, part_sems, 1, {"par": par_peer(0)}).wait_send()

    @pl.when(jnp.logical_not(owns_last))
    def _():
        parts(n_par - 1).wait_send()

    panel_all().wait_send()
    each(n_arc - 1, lambda i: gram_copy(i).wait_send())
    all_all().wait_send()
    fwd.wait_send()
    obs_copy().wait_send()
    sibling_panel_copy().wait_send()

    for t in range(4):
        one_copy(t).wait_send()
    for t in range(2):
        for h in range(2):
            two_copy(t, h).wait_send()
            each(n_arc - 1, lambda i: out_copy(t, h, i).wait())


def shards(observations, arc_mask, panel_owner):
    n_arc, n_par = lax.axis_size("arc"), lax.axis_size("par")
    rows, cols = observations.shape
    order = 2 * PANEL
    share = rows // n_par
    width = cols // 16
    tiles = order // TILE
    slice_rows = tiles * (tiles + 1) // 2 * TILE // (2 * n_par)

    def pair(count):
        return pltpu.SemaphoreType.DMA((2, count))

    return pl.pallas_call(
        functools.partial(kernel, n_arc, n_par),
        out_shape=jax.ShapeDtypeStruct((order // n_arc, cols), F32),
        in_specs=[pl.BlockSpec(memory_space=pl.ANY)] * 3,
        out_specs=pl.BlockSpec(memory_space=pltpu.VMEM),
        scratch_shapes=[
            pltpu.VMEM((rows, cols), F32),
            pltpu.SMEM(arc_mask.shape, jnp.int32),
            pltpu.SMEM(panel_owner.shape, jnp.int32),
            pltpu.VMEM((rows, order), F32),
            pltpu.VMEM((n_par - 1, share, order), F32),
            pltpu.VMEM((rows, order), F32),
            pltpu.VMEM((rows, cols // 2), F32),
            pltpu.VMEM((rows, order), F32),
            pltpu.VMEM((order, rows), F32),
            pltpu.VMEM((order, 6 * rows), BF16),
            pltpu.VMEM((2 * slice_rows, TILE), F32),
            pltpu.VMEM((n_arc - 1, slice_rows, TILE), F32),
            pltpu.VMEM((n_par, 2, slice_rows, TILE), F32),
            pltpu.VMEM((order, order), F32),
            pltpu.VMEM((8, order, width), F32),
            pltpu.VMEM((4, order, width), F32),
            pltpu.VMEM((2, order, width), F32),
            pltpu.VMEM((2, order, width), F32),
            pltpu.SemaphoreType.DMA((3,)),
            pair(2),
            pair(1),
            pair(n_arc - 1),
            pair(1),
            pair(3),
            pair(4),
            pair(4),
            pair(4 * (n_arc - 1)),
        ],
        compiler_params=pltpu.CompilerParams(
            collective_id=0, has_side_effects=True, vmem_limit_bytes=60 << 20
        ),
        name="info_rows",
    )(observations, arc_mask, panel_owner)


def solution(mesh):
    return jax.shard_map(
        shards,
        mesh=mesh,
        in_specs=(P("arc", "par"), P("arc", "par"), P()),
        out_specs=P("arc", "par"),
        check_vma=False,
    )
```

```python
import functools
import math

import jax
import jax.numpy as jnp
from jax import lax
from jax.experimental import pallas as pl
from jax.experimental.pallas import tpu as pltpu
from jax.sharding import PartitionSpec as P

PANEL = 256
BLK = 128
TILE = 128
HIGHEST = lax.Precision.HIGHEST
MESH = pl.DeviceIdType.MESH
F32 = jnp.float32
BF16 = jnp.bfloat16


def dot_nt(left, right):
    return lax.dot_general(left, right, (((1,), (1,)), ((), ())), precision=HIGHEST, preferred_element_type=F32)


def dot_nn(left, right):
    return jnp.dot(left, right, precision=HIGHEST, preferred_element_type=F32)


def halves(value):
    high = value.astype(BF16)
    return high, (value - high.astype(F32)).astype(BF16)


def tile_inverse(tile, width=8):
    lanes = lax.broadcasted_iota(jnp.int32, (8, TILE), 1)
    subl = lax.broadcasted_iota(jnp.int32, (8, TILE), 0)
    zero = jnp.zeros((8, TILE), F32)
    done = []
    tail = tile
    for start in range(0, TILE, width):
        base = start // 8
        size = TILE - 8 * base - 8
        head, tail = tail[:8], tail[8:]
        tail_lanes = lax.broadcasted_iota(jnp.int32, (size, TILE), 1) if size else None
        head_cols = [jnp.broadcast_to(head[:, start + c:start + c + 1], (8, TILE)) for c in range(width)]
        tail_cols = [jnp.broadcast_to(tail[:, start + c:start + c + 1], (size, TILE)) for c in range(width)] if size else None
        for c in range(width):
            col = start + c
            pivot = jnp.broadcast_to(head_cols[c][c:c + 1, :], (8, TILE))
            inv = 1.0 / pivot
            on_col = lanes == col
            prow = jnp.where(on_col, inv, jnp.broadcast_to(head[c:c + 1, :], (8, TILE)) * inv)
            below = subl > c
            mult = jnp.where(below, head_cols[c], zero)
            coefs = [jnp.broadcast_to(head_cols[d][c:c + 1, :], (8, TILE)) * inv for d in range(c + 1, width)]
            for d in range(c + 1, width):
                head_cols[d] = head_cols[d] - mult * coefs[d - c - 1]
            head = jnp.where(on_col, jnp.where(below, zero, jnp.where(subl == c, pivot, head)), head) - mult * prow
            if size:
                for d in range(c + 1, width):
                    tail_cols[d] = tail_cols[d] - tail_cols[c] * jnp.broadcast_to(coefs[d - c - 1][:1], (size, TILE))
                tail = jnp.where(tail_lanes == col, 0.0, tail) - tail_cols[c] * jnp.broadcast_to(prow[:1], (size, TILE))
        on_diag = lanes == subl + start
        diag = jnp.sum(jnp.where(on_diag, head, zero), axis=1, keepdims=True)
        scaled = jnp.where(on_diag, 1.0, head) * lax.rsqrt(diag)
        done.append(jnp.where(lanes <= subl + start, scaled, zero))
    return jnp.concatenate(done, 0)


def factor_step(ref, k, count):
    low, top = k * TILE, (k + 1) * TILE
    inv = tile_inverse(ref[low:top, low:top])
    ref[low:top, low:top] = inv
    if k:
        ref[low:top, :low] = dot_nn(inv, ref[low:top, :low])
    if k + 1 < count:
        below = dot_nt(ref[top:, low:top], inv)
        for i in range(k + 1, count):
            part = below[(i - k - 1) * TILE:(i - k) * TILE]
            ref[i * TILE:(i + 1) * TILE, top:(i + 1) * TILE] -= dot_nt(part, below[:(i - k) * TILE])
        if k:
            ref[top:, :low] -= dot_nn(below, ref[low:top, :low])
        ref[top:, low:top] = -dot_nn(below, inv)


def kernel(
    n_arc, n_par,
    obs_hbm, mask_hbm, owner_hbm, out_ref,
    obs_ref, mask_ref, owner_ref,
    part_ref, piece_ref, panel_ref, other_obs_ref, other_turned_ref, turned_ref, stack_ref,
    gram_ref, gram_piece_ref, gram_all_ref, fac_ref,
    sums_ref, from_one_ref, from_two_ref, result_ref,
    load_sems, part_sems, panel_sems, gram_sems, all_sems, core_sems, one_sems, two_sems, out_sems,
):
    rows, cols = obs_ref.shape
    order = 2 * PANEL
    share = rows // n_par
    slice_rows = gram_piece_ref.shape[1]
    width = cols // 16
    out_rows = out_ref.shape[0]
    tiles = order // TILE
    chips = n_arc // 2
    scale = 1.0 / math.sqrt(rows * n_arc)
    arc = lax.axis_index("arc")
    par = lax.axis_index("par")
    chip = arc // 2
    core = arc % 2

    def send(src, dst, sems, slot, target):
        return pltpu.make_async_remote_copy(
            src_ref=src, dst_ref=dst, send_sem=sems.at[0, slot], recv_sem=sems.at[1, slot],
            device_id=target, device_id_type=MESH,
        )

    def each(count, body):
        lax.fori_loop(0, count, lambda i, carry: (body(i), carry)[1], 0)

    def par_peer(i):
        return lax.rem(par + lax.rem(i * 4, n_par - 1) + 1, n_par)

    def arc_peer(i):
        return lax.rem(arc + i + 1, n_arc)

    sibling = {"arc": arc + 1 - 2 * core}
    loads = [
        pltpu.make_async_copy(src, dst, load_sems.at[i])
        for i, (src, dst) in enumerate([(mask_hbm, mask_ref), (owner_hbm, owner_ref), (obs_hbm, obs_ref)])
    ]
    for load in loads:
        load.start()

    barrier = pltpu.get_barrier_semaphore()
    each(n_par - 1, lambda i: pl.semaphore_signal(barrier, inc=1, device_id={"par": par_peer(i)}, device_id_type=MESH))
    each(n_arc - 1, lambda i: pl.semaphore_signal(barrier, inc=1, device_id={"arc": arc_peer(i)}, device_id_type=MESH))
    for load in loads:
        load.wait()

    held = cols // PANEL
    last = n_par * held - 1
    last_first = owner_ref[0] == last
    other = jnp.where(last_first, owner_ref[1], owner_ref[0])
    chosen = [jnp.where(other == par * held + b, 1.0, 0.0) for b in range(held)]
    for half in range(PANEL // BLK):
        for band in range(rows // BLK):
            low, top = band * BLK, (band + 1) * BLK
            total = jnp.zeros((BLK, BLK), F32)
            for b in range(held):
                block = b * (PANEL // BLK) + half
                left, right = block * BLK, (block + 1) * BLK
                masked = obs_ref[low:top, left:right] * mask_ref[band, block].astype(F32)
                obs_ref[low:top, left:right] = masked
                total = total + masked * chosen[b]
            part_ref[low:top, half * BLK:(half + 1) * BLK] = total

    pl.semaphore_wait(barrier, n_par + n_arc - 2)

    def share_of(device):
        return pl.ds(pl.multiple_of(device * share, 8), share)

    def part_copy(i):
        peer = par_peer(i)
        return send(part_ref.at[share_of(peer), :PANEL], piece_ref.at[i, :, :PANEL], part_sems, 0, {"par": peer})

    def both_copy(i):
        peer = par_peer(i)
        return send(part_ref.at[share_of(peer)], piece_ref.at[i], part_sems, 1, {"par": peer})

    def parts(count):
        some = piece_ref.at[:count, :, :PANEL]
        return send(some, some, part_sems, 0, {"par": par_peer(0)})

    def obs_copy():
        there = pl.ds(pl.multiple_of((1 - core) * (cols // 2), BLK), cols // 2)
        return send(obs_ref.at[:, there], other_obs_ref, core_sems, 0, sibling)

    def sibling_turned_copy():
        return send(turned_ref, other_turned_ref, core_sems, 1, sibling)

    owns_last = par == n_par - 1
    own_share = share_of(par)

    @pl.when(owns_last)
    def _():
        part_ref[:, PANEL:] = obs_ref[:, cols - PANEL:]
        each(n_par - 1, lambda i: both_copy(i).start())

    @pl.when(jnp.logical_not(owns_last))
    def _():
        each(n_par - 1, lambda i: part_copy(i).start())

    obs_copy().start()

    @pl.when(owns_last)
    def _():
        parts(n_par - 1).wait_recv()
        panel_ref[own_share, PANEL:] = part_ref[own_share, PANEL:]

    @pl.when(jnp.logical_not(owns_last))
    def _():
        parts(n_par - 2).wait_recv()
        slot = lax.rem(par * 4, n_par - 1)
        both_copy(slot).wait_recv()
        panel_ref[own_share, PANEL:] = piece_ref[slot, :, PANEL:]

    total = part_ref[own_share, :PANEL]
    for i in range(n_par - 1):
        total = total + piece_ref[i, :, :PANEL]
    panel_ref[own_share, :PANEL] = total

    def panel_copy(i):
        return send(panel_ref.at[own_share], panel_ref.at[own_share], panel_sems, 0, {"par": par_peer(i)})

    def panel_all():
        others = panel_ref.at[:share * (n_par - 1)]
        return send(others, others, panel_sems, 0, {"par": par_peer(0)})

    each(n_par - 1, lambda i: panel_copy(i).start())
    panel_all().wait_recv()

    def in_order(ref):
        one, two = ref[:, :PANEL], ref[:, PANEL:]
        return jnp.concatenate([jnp.where(last_first, two, one), jnp.where(last_first, one, two)], 1)

    panel = in_order(panel_ref)
    turned = panel.T
    turned_ref[...] = turned
    sibling_turned_copy().start()
    band_rows = TILE // n_par
    picked = [turned_ref[pl.ds(pl.multiple_of(i * TILE + par * band_rows, 8), band_rows), :] for i in range(tiles)]
    gram_rows = dot_nn(jnp.concatenate(picked, 0), panel)
    for i in range(tiles):
        for j in range(i + 1):
            at = (i * (i + 1) // 2 + j) * band_rows
            gram_ref[at:at + band_rows, :] = gram_rows[i * band_rows:(i + 1) * band_rows, j * TILE:(j + 1) * TILE]

    def gram_copy(i):
        peer = arc_peer(i)
        at = pl.multiple_of(peer % 2 * slice_rows, 8)
        return send(gram_ref.at[pl.ds(at, slice_rows)], gram_piece_ref.at[i], gram_sems, i, {"arc": peer})

    each(n_arc - 1, lambda i: gram_copy(i).start())

    def fill_stack(at, turned_panel):
        high, low = halves(turned_panel)
        stack_ref[:, at:at + 3 * rows] = jnp.concatenate([high, high, low], 1)

    fill_stack(0, turned)

    def owner_chip(t):
        side = t % 2
        across = chips - 1 - chip
        beside = chip + 1 - 2 * (chip % 2)
        return [
            (lax.rem(chip + 2, chips), lax.rem(chip + 2, chips)),
            (beside, across),
            (across, beside),
            (chip, chip),
        ][t // 2][side]

    def column_of(t):
        return pl.multiple_of(((t % 2) * 4 + owner_chip(t)) * width, BLK)

    def product(at, columns):
        up, down = halves(columns)
        return jnp.dot(stack_ref[:, at:at + 3 * rows], jnp.concatenate([up, down, up], 0), preferred_element_type=F32)

    def own_product(t):
        return product(0, obs_ref[:, pl.ds(pl.multiple_of(core * (cols // 2) + column_of(t), BLK), width)])

    def other_product(t):
        return product(3 * rows, other_obs_ref[:, pl.ds(column_of(t), width)])

    def one_copy(t):
        to = (chip + 1 - 2 * (chip % 2)) if t % 2 == 0 else (chips - 1 - chip)
        return send(sums_ref.at[t], from_one_ref.at[t], one_sems, t, {"arc": 2 * to + core})

    for t in range(2):
        sums_ref[t] = own_product(t)
    obs_copy().wait_recv()
    sibling_turned_copy().wait_recv()
    fill_stack(3 * rows, other_turned_ref[...])
    for t in range(4):
        own = sums_ref[t] if t < 2 else own_product(t)
        sums_ref[t] = own + other_product(t)
        one_copy(t).start()

    each(n_arc - 1, lambda i: gram_copy(i).wait_recv())
    own_at = pl.multiple_of(core * slice_rows, 8)
    gram_total = gram_ref[pl.ds(own_at, slice_rows), :]
    for i in range(n_arc - 1):
        gram_total = gram_total + gram_piece_ref[i]
    gram_all_ref[par, core] = gram_total

    def all_copy(i):
        here = gram_all_ref.at[par, core]
        return send(here, here, all_sems, 0, {"par": par_peer(i)})

    def all_all():
        others = gram_all_ref.at[:n_par - 1, core]
        return send(others, others, all_sems, 0, {"par": par_peer(0)})

    each(n_par - 1, lambda i: all_copy(i).start())

    for t in range(4, 8):
        sums_ref[t] = own_product(t) + other_product(t)

    all_all().wait_recv()
    fwd = send(gram_all_ref.at[:, core], gram_all_ref.at[:, core], core_sems, 2, sibling)
    fwd.start()
    fwd.wait_recv()
    for i in range(tiles):
        for j in range(i + 1):
            half, at = divmod((i * (i + 1) // 2 + j) * band_rows, slice_rows)
            block = gram_all_ref[:, half, at:at + band_rows, :].reshape(TILE, TILE)
            fac_ref[i * TILE:(i + 1) * TILE, j * TILE:(j + 1) * TILE] = block
        if i + 1 < tiles:
            fac_ref[i * TILE:(i + 1) * TILE, (i + 1) * TILE:] = jnp.zeros((TILE, order - (i + 1) * TILE), F32)

    part = width // 2

    def two_copy(t, h):
        to = (chips - 1 - chip) if t % 2 == 0 else (chip + 1 - 2 * (chip % 2))
        columns = pl.ds(h * part, part)
        return send(
            sums_ref.at[4 + t, :, columns], from_two_ref.at[t, :, columns], two_sems, 2 * t + h, {"arc": 2 * to + core}
        )

    for k in range(tiles):
        factor_step(fac_ref, k, tiles)
        if k == 1:
            for t in range(2):
                one_copy(t).wait_recv()
                sums_ref[4 + t] = sums_ref[4 + t] + from_one_ref[t]
                two_copy(t, 0).start()
            for t in range(2):
                two_copy(t, 1).start()

    def out_column(t, h):
        return pl.multiple_of(core * (cols // 2) + column_of(6 + t) + h * part, BLK)

    def out_copy(t, h, i):
        peer = arc_peer(i)
        src = result_ref.at[t, pl.ds(pl.multiple_of(peer * out_rows, 8), out_rows), h * part:(h + 1) * part]
        dst = out_ref.at[:, pl.ds(out_column(t, h), part)]
        return send(src, dst, out_sems, (2 * t + h) * (n_arc - 1) + i, {"arc": peer})

    for h in range(2):
        for t in range(2):
            left, right = h * part, (h + 1) * part
            if h == 0:
                one_copy(2 + t).wait_recv()
            two_copy(t, h).wait_recv()
            whole = sums_ref[6 + t, :, left:right] + from_one_ref[2 + t, :, left:right] + from_two_ref[t, :, left:right]
            for i in range(tiles):
                depth = (i + 1) * TILE
                result_ref[t, i * TILE:depth, left:right] = dot_nn(fac_ref[i * TILE:depth, :depth], whole[:depth]) * scale
            each(n_arc - 1, lambda i: out_copy(t, h, i).start())
            out_ref[:, pl.ds(out_column(t, h), part)] = result_ref[
                t, pl.ds(pl.multiple_of(arc * out_rows, 8), out_rows), left:right
            ]

    @pl.when(owns_last)
    def _():
        send(piece_ref, piece_ref, part_sems, 1, {"par": par_peer(0)}).wait_send()

    @pl.when(jnp.logical_not(owns_last))
    def _():
        parts(n_par - 1).wait_send()

    panel_all().wait_send()
    each(n_arc - 1, lambda i: gram_copy(i).wait_send())
    all_all().wait_send()
    fwd.wait_send()
    obs_copy().wait_send()
    sibling_turned_copy().wait_send()

    for t in range(4):
        one_copy(t).wait_send()
    for t in range(2):
        for h in range(2):
            two_copy(t, h).wait_send()
            each(n_arc - 1, lambda i: out_copy(t, h, i).wait())


def shards(observations, arc_mask, panel_owner):
    n_arc, n_par = lax.axis_size("arc"), lax.axis_size("par")
    rows, cols = observations.shape
    order = 2 * PANEL
    share = rows // n_par
    width = cols // 16
    tiles = order // TILE
    slice_rows = tiles * (tiles + 1) // 2 * TILE // (2 * n_par)

    def pair(count):
        return pltpu.SemaphoreType.DMA((2, count))

    return pl.pallas_call(
        functools.partial(kernel, n_arc, n_par),
        out_shape=jax.ShapeDtypeStruct((order // n_arc, cols), F32),
        in_specs=[pl.BlockSpec(memory_space=pl.ANY)] * 3,
        out_specs=pl.BlockSpec(memory_space=pltpu.VMEM),
        scratch_shapes=[
            pltpu.VMEM((rows, cols), F32),
            pltpu.SMEM(arc_mask.shape, jnp.int32),
            pltpu.SMEM(panel_owner.shape, jnp.int32),
            pltpu.VMEM((rows, order), F32),
            pltpu.VMEM((n_par - 1, share, order), F32),
            pltpu.VMEM((rows, order), F32),
            pltpu.VMEM((rows, cols // 2), F32),
            pltpu.VMEM((order, rows), F32),
            pltpu.VMEM((order, rows), F32),
            pltpu.VMEM((order, 6 * rows), BF16),
            pltpu.VMEM((2 * slice_rows, TILE), F32),
            pltpu.VMEM((n_arc - 1, slice_rows, TILE), F32),
            pltpu.VMEM((n_par, 2, slice_rows, TILE), F32),
            pltpu.VMEM((order, order), F32),
            pltpu.VMEM((8, order, width), F32),
            pltpu.VMEM((4, order, width), F32),
            pltpu.VMEM((2, order, width), F32),
            pltpu.VMEM((2, order, width), F32),
            pltpu.SemaphoreType.DMA((3,)),
            pair(2),
            pair(1),
            pair(n_arc - 1),
            pair(1),
            pair(3),
            pair(4),
            pair(4),
            pair(4 * (n_arc - 1)),
        ],
        compiler_params=pltpu.CompilerParams(
            collective_id=0, has_side_effects=True, vmem_limit_bytes=60 << 20
        ),
        name="info_rows",
    )(observations, arc_mask, panel_owner)


def solution(mesh):
    return jax.shard_map(
        shards,
        mesh=mesh,
        in_specs=(P("arc", "par"), P("arc", "par"), P()),
        out_specs=P("arc", "par"),
        check_vma=False,
    )
```

```python
import functools
import math

import jax
import jax.numpy as jnp
from jax import lax
from jax.experimental import pallas as pl
from jax.experimental.pallas import tpu as pltpu
from jax.sharding import PartitionSpec as P

PANEL = 256
BLK = 128
TILE = 128
HIGHEST = lax.Precision.HIGHEST
MESH = pl.DeviceIdType.MESH
F32 = jnp.float32
BF16 = jnp.bfloat16


def dot_nt(left, right):
    return lax.dot_general(left, right, (((1,), (1,)), ((), ())), precision=HIGHEST, preferred_element_type=F32)


def dot_nn(left, right):
    return jnp.dot(left, right, precision=HIGHEST, preferred_element_type=F32)


def halves(value):
    high = value.astype(BF16)
    return high, (value - high.astype(F32)).astype(BF16)


def tile_inverse(tile, width=8):
    lanes = lax.broadcasted_iota(jnp.int32, (8, TILE), 1)
    subl = lax.broadcasted_iota(jnp.int32, (8, TILE), 0)
    zero = jnp.zeros((8, TILE), F32)
    done = []
    tail = tile
    for start in range(0, TILE, width):
        base = start // 8
        size = TILE - 8 * base - 8
        head, tail = tail[:8], tail[8:]
        tail_lanes = lax.broadcasted_iota(jnp.int32, (size, TILE), 1) if size else None
        head_cols = [jnp.broadcast_to(head[:, start + c:start + c + 1], (8, TILE)) for c in range(width)]
        tail_cols = [jnp.broadcast_to(tail[:, start + c:start + c + 1], (size, TILE)) for c in range(width)] if size else None
        for c in range(width):
            col = start + c
            pivot = jnp.broadcast_to(head_cols[c][c:c + 1, :], (8, TILE))
            inv = 1.0 / pivot
            on_col = lanes == col
            prow = jnp.where(on_col, inv, jnp.broadcast_to(head[c:c + 1, :], (8, TILE)) * inv)
            below = subl > c
            mult = jnp.where(below, head_cols[c], zero)
            coefs = [jnp.broadcast_to(head_cols[d][c:c + 1, :], (8, TILE)) * inv for d in range(c + 1, width)]
            for d in range(c + 1, width):
                head_cols[d] = head_cols[d] - mult * coefs[d - c - 1]
            head = jnp.where(on_col, jnp.where(below, zero, jnp.where(subl == c, pivot, head)), head) - mult * prow
            if size:
                for d in range(c + 1, width):
                    tail_cols[d] = tail_cols[d] - tail_cols[c] * jnp.broadcast_to(coefs[d - c - 1][:1], (size, TILE))
                tail = jnp.where(tail_lanes == col, 0.0, tail) - tail_cols[c] * jnp.broadcast_to(prow[:1], (size, TILE))
        on_diag = lanes == subl + start
        diag = jnp.sum(jnp.where(on_diag, head, zero), axis=1, keepdims=True)
        scaled = jnp.where(on_diag, 1.0, head) * lax.rsqrt(diag)
        done.append(jnp.where(lanes <= subl + start, scaled, zero))
    return jnp.concatenate(done, 0)


def factor_step(ref, k, count):
    low, top = k * TILE, (k + 1) * TILE
    inv = tile_inverse(ref[low:top, low:top])
    ref[low:top, low:top] = inv
    if k:
        ref[low:top, :low] = dot_nn(inv, ref[low:top, :low])
    if k + 1 < count:
        below = dot_nt(ref[top:, low:top], inv)
        for i in range(k + 1, count):
            part = below[(i - k - 1) * TILE:(i - k) * TILE]
            ref[i * TILE:(i + 1) * TILE, top:(i + 1) * TILE] -= dot_nt(part, below[:(i - k) * TILE])
        if k:
            ref[top:, :low] -= dot_nn(below, ref[low:top, :low])
        ref[top:, low:top] = -dot_nn(below, inv)


def kernel(
    n_arc, n_par,
    obs_hbm, mask_hbm, owner_hbm, out_ref,
    obs_ref, mask_ref, owner_ref,
    part_ref, piece_ref, panel_ref, other_obs_ref, other_panel_ref, turned_ref, stack_ref,
    gram_ref, gram_piece_ref, gram_all_ref, fac_ref,
    sums_ref, from_one_ref, from_two_ref, result_ref,
    load_sems, part_sems, panel_sems, gram_sems, all_sems, core_sems, one_sems, two_sems, out_sems,
):
    rows, cols = obs_ref.shape
    order = 2 * PANEL
    share = rows // n_par
    slice_rows = gram_piece_ref.shape[1]
    width = cols // 16
    out_rows = out_ref.shape[0]
    tiles = order // TILE
    chips = n_arc // 2
    scale = 1.0 / math.sqrt(rows * n_arc)
    arc = lax.axis_index("arc")
    par = lax.axis_index("par")
    chip = arc // 2
    core = arc % 2

    def send(src, dst, sems, slot, target):
        return pltpu.make_async_remote_copy(
            src_ref=src, dst_ref=dst, send_sem=sems.at[0, slot], recv_sem=sems.at[1, slot],
            device_id=target, device_id_type=MESH,
        )

    def each(count, body):
        lax.fori_loop(0, count, lambda i, carry: (body(i), carry)[1], 0)

    def par_peer(i):
        return lax.rem(par + lax.rem(i * 4, n_par - 1) + 1, n_par)

    def arc_peer(i):
        return lax.rem(arc + i + 1, n_arc)

    sibling = {"arc": arc + 1 - 2 * core}
    loads = [
        pltpu.make_async_copy(src, dst, load_sems.at[i])
        for i, (src, dst) in enumerate([(mask_hbm, mask_ref), (owner_hbm, owner_ref), (obs_hbm, obs_ref)])
    ]
    for load in loads:
        load.start()

    barrier = pltpu.get_barrier_semaphore()
    each(n_par - 1, lambda i: pl.semaphore_signal(barrier, inc=1, device_id={"par": par_peer(i)}, device_id_type=MESH))
    each(n_arc - 1, lambda i: pl.semaphore_signal(barrier, inc=1, device_id={"arc": arc_peer(i)}, device_id_type=MESH))
    for load in loads:
        load.wait()

    held = cols // PANEL
    last = n_par * held - 1
    last_first = owner_ref[0] == last
    other = jnp.where(last_first, owner_ref[1], owner_ref[0])
    chosen = [jnp.where(other == par * held + b, 1.0, 0.0) for b in range(held)]
    for half in range(PANEL // BLK):
        for band in range(rows // BLK):
            low, top = band * BLK, (band + 1) * BLK
            total = jnp.zeros((BLK, BLK), F32)
            for b in range(held):
                block = b * (PANEL // BLK) + half
                left, right = block * BLK, (block + 1) * BLK
                masked = obs_ref[low:top, left:right] * mask_ref[band, block].astype(F32)
                obs_ref[low:top, left:right] = masked
                total = total + masked * chosen[b]
            part_ref[low:top, half * BLK:(half + 1) * BLK] = total

    pl.semaphore_wait(barrier, n_par + n_arc - 2)

    def share_of(device):
        return pl.ds(pl.multiple_of(device * share, 8), share)

    def part_copy(i):
        peer = par_peer(i)
        return send(part_ref.at[share_of(peer), :PANEL], piece_ref.at[i, :, :PANEL], part_sems, 0, {"par": peer})

    def both_copy(i):
        peer = par_peer(i)
        return send(part_ref.at[share_of(peer)], piece_ref.at[i], part_sems, 1, {"par": peer})

    def parts(count):
        some = piece_ref.at[:count, :, :PANEL]
        return send(some, some, part_sems, 0, {"par": par_peer(0)})

    def obs_copy():
        there = pl.ds(pl.multiple_of((1 - core) * (cols // 2), BLK), cols // 2)
        return send(obs_ref.at[:, there], other_obs_ref, core_sems, 0, sibling)

    def sibling_panel_copy():
        return send(panel_ref, other_panel_ref, core_sems, 1, sibling)

    owns_last = par == n_par - 1
    own_share = share_of(par)

    @pl.when(owns_last)
    def _():
        part_ref[:, PANEL:] = obs_ref[:, cols - PANEL:]
        each(n_par - 1, lambda i: both_copy(i).start())

    @pl.when(jnp.logical_not(owns_last))
    def _():
        each(n_par - 1, lambda i: part_copy(i).start())

    obs_copy().start()

    @pl.when(owns_last)
    def _():
        parts(n_par - 1).wait_recv()
        panel_ref[own_share, PANEL:] = part_ref[own_share, PANEL:]

    @pl.when(jnp.logical_not(owns_last))
    def _():
        parts(n_par - 2).wait_recv()
        slot = lax.rem(par * 4, n_par - 1)
        both_copy(slot).wait_recv()
        panel_ref[own_share, PANEL:] = piece_ref[slot, :, PANEL:]

    total = part_ref[own_share, :PANEL]
    for i in range(n_par - 1):
        total = total + piece_ref[i, :, :PANEL]
    panel_ref[own_share, :PANEL] = total

    def panel_copy(i):
        return send(panel_ref.at[own_share], panel_ref.at[own_share], panel_sems, 0, {"par": par_peer(i)})

    def panel_all():
        others = panel_ref.at[:share * (n_par - 1)]
        return send(others, others, panel_sems, 0, {"par": par_peer(0)})

    each(n_par - 1, lambda i: panel_copy(i).start())
    panel_all().wait_recv()
    sibling_panel_copy().start()

    def in_order(ref):
        one, two = ref[:, :PANEL], ref[:, PANEL:]
        return jnp.concatenate([jnp.where(last_first, two, one), jnp.where(last_first, one, two)], 1)

    panel = in_order(panel_ref)
    turned = panel.T
    turned_ref[...] = turned
    band_rows = TILE // n_par
    picked = [turned_ref[pl.ds(pl.multiple_of(i * TILE + par * band_rows, 8), band_rows), :] for i in range(tiles)]
    gram_rows = dot_nn(jnp.concatenate(picked, 0), panel)
    for i in range(tiles):
        for j in range(i + 1):
            at = (i * (i + 1) // 2 + j) * band_rows
            gram_ref[at:at + band_rows, :] = gram_rows[i * band_rows:(i + 1) * band_rows, j * TILE:(j + 1) * TILE]

    def gram_copy(i):
        peer = arc_peer(i)
        at = pl.multiple_of(peer % 2 * slice_rows, 8)
        return send(gram_ref.at[pl.ds(at, slice_rows)], gram_piece_ref.at[i], gram_sems, i, {"arc": peer})

    each(n_arc - 1, lambda i: gram_copy(i).start())

    def fill_stack(at, turned_panel):
        high, low = halves(turned_panel)
        stack_ref[:, at:at + 3 * rows] = jnp.concatenate([high, high, low], 1)

    fill_stack(0, turned)

    def owner_chip(t):
        side = t % 2
        across = chips - 1 - chip
        beside = chip + 1 - 2 * (chip % 2)
        return [
            (lax.rem(chip + 2, chips), lax.rem(chip + 2, chips)),
            (beside, across),
            (across, beside),
            (chip, chip),
        ][t // 2][side]

    def column_of(t):
        return pl.multiple_of(((t % 2) * 4 + owner_chip(t)) * width, BLK)

    def product(at, columns):
        up, down = halves(columns)
        return jnp.dot(stack_ref[:, at:at + 3 * rows], jnp.concatenate([up, down, up], 0), preferred_element_type=F32)

    def own_product(t):
        return product(0, obs_ref[:, pl.ds(pl.multiple_of(core * (cols // 2) + column_of(t), BLK), width)])

    def other_product(t):
        return product(3 * rows, other_obs_ref[:, pl.ds(column_of(t), width)])

    def one_copy(t):
        to = (chip + 1 - 2 * (chip % 2)) if t % 2 == 0 else (chips - 1 - chip)
        return send(sums_ref.at[t], from_one_ref.at[t], one_sems, t, {"arc": 2 * to + core})

    for t in range(4):
        sums_ref[t] = own_product(t)
    obs_copy().wait_recv()
    sibling_panel_copy().wait_recv()
    fill_stack(3 * rows, in_order(other_panel_ref).T)
    for t in range(4):
        sums_ref[t] = sums_ref[t] + other_product(t)
        one_copy(t).start()

    each(n_arc - 1, lambda i: gram_copy(i).wait_recv())
    own_at = pl.multiple_of(core * slice_rows, 8)
    gram_total = gram_ref[pl.ds(own_at, slice_rows), :]
    for i in range(n_arc - 1):
        gram_total = gram_total + gram_piece_ref[i]
    gram_all_ref[par, core] = gram_total

    def all_copy(i):
        here = gram_all_ref.at[par, core]
        return send(here, here, all_sems, 0, {"par": par_peer(i)})

    def all_all():
        others = gram_all_ref.at[:n_par - 1, core]
        return send(others, others, all_sems, 0, {"par": par_peer(0)})

    each(n_par - 1, lambda i: all_copy(i).start())

    for t in range(4, 8):
        sums_ref[t] = own_product(t) + other_product(t)

    all_all().wait_recv()
    fwd = send(gram_all_ref.at[:, core], gram_all_ref.at[:, core], core_sems, 2, sibling)
    fwd.start()
    fwd.wait_recv()
    for i in range(tiles):
        for j in range(i + 1):
            half, at = divmod((i * (i + 1) // 2 + j) * band_rows, slice_rows)
            block = gram_all_ref[:, half, at:at + band_rows, :].reshape(TILE, TILE)
            fac_ref[i * TILE:(i + 1) * TILE, j * TILE:(j + 1) * TILE] = block
        if i + 1 < tiles:
            fac_ref[i * TILE:(i + 1) * TILE, (i + 1) * TILE:] = jnp.zeros((TILE, order - (i + 1) * TILE), F32)

    part = width // 2

    def two_copy(t, h):
        to = (chips - 1 - chip) if t % 2 == 0 else (chip + 1 - 2 * (chip % 2))
        columns = pl.ds(h * part, part)
        return send(
            sums_ref.at[4 + t, :, columns], from_two_ref.at[t, :, columns], two_sems, 2 * t + h, {"arc": 2 * to + core}
        )

    for k in range(tiles):
        factor_step(fac_ref, k, tiles)
        if k == 0:
            for t in range(2):
                one_copy(t).wait_recv()
                sums_ref[4 + t] = sums_ref[4 + t] + from_one_ref[t]
                two_copy(t, 0).start()
            for t in range(2):
                two_copy(t, 1).start()

    def out_column(t, h):
        return pl.multiple_of(core * (cols // 2) + column_of(6 + t) + h * part, BLK)

    def out_copy(t, h, i):
        peer = arc_peer(i)
        src = result_ref.at[t, pl.ds(pl.multiple_of(peer * out_rows, 8), out_rows), h * part:(h + 1) * part]
        dst = out_ref.at[:, pl.ds(out_column(t, h), part)]
        return send(src, dst, out_sems, (2 * t + h) * (n_arc - 1) + i, {"arc": peer})

    for h in range(2):
        for t in range(2):
            left, right = h * part, (h + 1) * part
            if h == 0:
                one_copy(2 + t).wait_recv()
            two_copy(t, h).wait_recv()
            whole = sums_ref[6 + t, :, left:right] + from_one_ref[2 + t, :, left:right] + from_two_ref[t, :, left:right]
            for i in range(tiles):
                depth = (i + 1) * TILE
                result_ref[t, i * TILE:depth, left:right] = dot_nn(fac_ref[i * TILE:depth, :depth], whole[:depth]) * scale
            each(n_arc - 1, lambda i: out_copy(t, h, i).start())
            out_ref[:, pl.ds(out_column(t, h), part)] = result_ref[
                t, pl.ds(pl.multiple_of(arc * out_rows, 8), out_rows), left:right
            ]

    @pl.when(owns_last)
    def _():
        send(piece_ref, piece_ref, part_sems, 1, {"par": par_peer(0)}).wait_send()

    @pl.when(jnp.logical_not(owns_last))
    def _():
        parts(n_par - 1).wait_send()

    panel_all().wait_send()
    each(n_arc - 1, lambda i: gram_copy(i).wait_send())
    all_all().wait_send()
    fwd.wait_send()
    obs_copy().wait_send()
    sibling_panel_copy().wait_send()

    for t in range(4):
        one_copy(t).wait_send()
    for t in range(2):
        for h in range(2):
            two_copy(t, h).wait_send()
            each(n_arc - 1, lambda i: out_copy(t, h, i).wait())


def shards(observations, arc_mask, panel_owner):
    n_arc, n_par = lax.axis_size("arc"), lax.axis_size("par")
    rows, cols = observations.shape
    order = 2 * PANEL
    share = rows // n_par
    width = cols // 16
    tiles = order // TILE
    slice_rows = tiles * (tiles + 1) // 2 * TILE // (2 * n_par)

    def pair(count):
        return pltpu.SemaphoreType.DMA((2, count))

    return pl.pallas_call(
        functools.partial(kernel, n_arc, n_par),
        out_shape=jax.ShapeDtypeStruct((order // n_arc, cols), F32),
        in_specs=[pl.BlockSpec(memory_space=pl.ANY)] * 3,
        out_specs=pl.BlockSpec(memory_space=pltpu.VMEM),
        scratch_shapes=[
            pltpu.VMEM((rows, cols), F32),
            pltpu.SMEM(arc_mask.shape, jnp.int32),
            pltpu.SMEM(panel_owner.shape, jnp.int32),
            pltpu.VMEM((rows, order), F32),
            pltpu.VMEM((n_par - 1, share, order), F32),
            pltpu.VMEM((rows, order), F32),
            pltpu.VMEM((rows, cols // 2), F32),
            pltpu.VMEM((rows, order), F32),
            pltpu.VMEM((order, rows), F32),
            pltpu.VMEM((order, 6 * rows), BF16),
            pltpu.VMEM((2 * slice_rows, TILE), F32),
            pltpu.VMEM((n_arc - 1, slice_rows, TILE), F32),
            pltpu.VMEM((n_par, 2, slice_rows, TILE), F32),
            pltpu.VMEM((order, order), F32),
            pltpu.VMEM((8, order, width), F32),
            pltpu.VMEM((4, order, width), F32),
            pltpu.VMEM((2, order, width), F32),
            pltpu.VMEM((2, order, width), F32),
            pltpu.SemaphoreType.DMA((3,)),
            pair(2),
            pair(1),
            pair(n_arc - 1),
            pair(1),
            pair(3),
            pair(4),
            pair(4),
            pair(4 * (n_arc - 1)),
        ],
        compiler_params=pltpu.CompilerParams(
            collective_id=0, has_side_effects=True, vmem_limit_bytes=60 << 20
        ),
        name="info_rows",
    )(observations, arc_mask, panel_owner)


def solution(mesh):
    return jax.shard_map(
        shards,
        mesh=mesh,
        in_specs=(P("arc", "par"), P("arc", "par"), P()),
        out_specs=P("arc", "par"),
        check_vma=False,
    )
```
